32 devices in a mesh: fsdp: 8 (over z, x), seq: 4 (over y, core).
Axes of the slice: x: 2, y: 2, z: 4, core: 2. Of those that a mesh axis runs over, the one named last changes fastest.
Arguments:
- frames_in: bfloat16 [8, 1024, 768], P('fsdp', 'seq'), may hold values from -6 to 6
- norm1_gain: bfloat16 [768], P('fsdp'), may hold values from 0.099609375 to 1.8984375
- norm1_bias: bfloat16 [768], P('fsdp'), may hold values from -1.75 to 1.75
- qkv_weight: bfloat16 [768, 2304], P('fsdp'), may hold values from -0.21875 to 0.21875
- query_bias: bfloat16 [768], P('fsdp'), may hold values from -3 to 3
- value_bias: bfloat16 [768], P('fsdp'), may hold values from -1.75 to 1.75
- out_weight: bfloat16 [768, 768], P('fsdp'), may hold values from -3 to 3
- out_bias: bfloat16 [768], P('fsdp'), may hold values from -1.75 to 1.75
- norm2_gain: bfloat16 [768], P('fsdp'), may hold values from 0.099609375 to 1.8984375
- norm2_bias: bfloat16 [768], P('fsdp'), may hold values from -1.75 to 1.75
- up_weight: bfloat16 [768, 3072], P('fsdp'), may hold values from -0.21875 to 0.21875
- up_bias: bfloat16 [3072], P('fsdp'), may hold values from -3 to 3
- down_weight: bfloat16 [3072, 768], P('fsdp'), may hold values from -0.109375 to 0.109375
- down_bias: bfloat16 [768], P('fsdp'), may hold values from -1.75 to 1.75
- cotangent: bfloat16 [8, 1024, 768], P('fsdp', 'seq'), may hold values from -6 to 6
Outputs:
- layer_out: bfloat16 [8, 1024, 768], P('fsdp', 'seq')
- input_grad: bfloat16 [8, 1024, 768], P('fsdp', 'seq')
- norm1_gain_grad: float32 [768], P('fsdp')
- norm1_bias_grad: float32 [768], P('fsdp')
- qkv_weight_grad: float32 [768, 2304], P('fsdp', 'seq')
- query_bias_grad: float32 [768], P('fsdp')
- value_bias_grad: float32 [768], P('fsdp')
- out_weight_grad: float32 [768, 768], P('fsdp', 'seq')
- out_bias_grad: float32 [768], P('fsdp')
- norm2_gain_grad: float32 [768], P('fsdp')
- norm2_bias_grad: float32 [768], P('fsdp')
- up_weight_grad: float32 [768, 3072], P('fsdp', 'seq')
- up_bias_grad: float32 [3072], P('fsdp')
- down_weight_grad: float32 [3072, 768], P('fsdp', 'seq')
- down_bias_grad: float32 [768], P('fsdp')
The draws below stay inside these ranges and needn't reach their ends.
All inputs are finite; a program needn't handle non-finite values.
Results may differ from the reference program's by a relative error of at most 0.012.
Values may be sent and summed in bfloat16 or wider, within the bound.
No kernel may reach another device: no remote copies, remote signals or barrier semaphores. Data moves between devices by JAX's collectives and lax.ppermute only.
A program may use at most 128 MiB of HBM per device.

```python
import math
import jax
import jax.numpy as jnp
from jax import lax

D = 768
H = 12
HD = 64
FF = 3072
FRAMES = 1024
CLIPS = 8
QBLOCK = 512


def block_scale(stream_key, dims, shards, least, largest):
    level, own = 1.0, jax.random.fold_in(stream_key, 6)
    for dim, shards_of in shards:
        draws = jnp.exp(jax.random.uniform(jax.random.fold_in(own, dim), (shards_of,), jnp.float32, least / len(shards), largest / len(shards)))
        level = level * jnp.repeat(draws, dims[dim] // shards_of).reshape([-1 if axis == dim else 1 for axis in range(len(dims))])
    return level


def centred(key, extent, width, bound, split=(), dtype=jnp.bfloat16):
    array = jax.random.normal(key, extent, jnp.float32) * width
    if len(split) > 0:
        array = block_scale(key, extent, split, -0.22, 0.18) * array
    return jnp.clip(array, min=-bound, max=bound).astype(dtype)


def setup_inputs(seed: int = 0) -> dict:
    keys = jax.random.split(jax.random.key(seed), 16)
    return {
        "frames_in": centred(keys[0], (CLIPS, FRAMES, D), 1.0, 6.0, ((0, 8), (1, 4))),
        "norm1_gain": jnp.clip(1.0 + 0.18 * jax.random.normal(keys[1], (D,), jnp.float32), 0.099609375, 1.8984375).astype(jnp.bfloat16),
        "norm1_bias": centred(keys[2], (D,), 0.3, 1.75, ((0, 8),)),
        "qkv_weight": centred(keys[3], (D, 3 * D), D ** -0.5, 0.21875, ((0, 8),)),
        "query_bias": centred(keys[4], (D,), 0.5, 3.0, ((0, 8),)),
        "value_bias": centred(keys[5], (D,), 0.3, 1.75, ((0, 8),)),
        "out_weight": centred(keys[6], (D, D), (max(6 * D // FRAMES, 1)) ** -0.5, 3.0, ((0, 8),)),
        "out_bias": centred(keys[7], (D,), 0.3, 1.75, ((0, 8),)),
        "norm2_gain": jnp.clip(1.0 + 0.18 * jax.random.normal(keys[8], (D,), jnp.float32), 0.099609375, 1.8984375).astype(jnp.bfloat16),
        "norm2_bias": centred(keys[9], (D,), 0.3, 1.75, ((0, 8),)),
        "up_weight": centred(keys[10], (D, FF), D ** -0.5, 0.21875, ((0, 8),)),
        "up_bias": centred(keys[11], (FF,), 0.5, 3.0, ((0, 8),)),
        "down_weight": centred(keys[12], (FF, D), FF ** -0.5, 0.109375, ((0, 8),)),
        "down_bias": centred(keys[13], (D,), 0.3, 1.75, ((0, 8),)),
        "cotangent": centred(keys[14], (CLIPS, FRAMES, D), 1.0, 6.0, ((0, 8), (1, 4))),
    }


@jax.custom_vjp
def low(v):
    return lax.optimization_barrier(v.astype(jnp.bfloat16)).astype(jnp.float32)

@jax.custom_vjp
def low_back(v):
    return v

def low_keep(v):
    return (low(v), None)

def low_pass(kept, grad):
    return (grad,)

def back_keep(v):
    return (v, None)

def back_low(kept, grad):
    return (low(grad),)
low.defvjp(low_keep, low_pass)
low_back.defvjp(back_keep, back_low)
epsilon = 1e-05
highest = lax.Precision.HIGHEST

def layer_norm(values, gain, shift):
    center = values - lax.optimization_barrier(jnp.mean(values, -1, keepdims=True))
    spread = lax.optimization_barrier(jnp.mean(center * center, -1, keepdims=True))
    return center * lax.rsqrt(spread + epsilon) * gain + shift

def forward(inputs, norm1_gain, norm1_bias, qkv_weight, query_bias, value_bias, out_weight, out_bias, norm2_gain, norm2_bias, up_weight, up_bias, down_weight, down_bias):
    group_size = inputs.shape[0]
    act_one = low(layer_norm(inputs, norm1_gain, norm1_bias))
    qkv_bias = jnp.concatenate([query_bias, jnp.zeros_like(query_bias), value_bias])
    projected = jnp.einsum('gfd,de->gfe', act_one, qkv_weight, precision=highest) + qkv_bias
    projected = low_back(low(projected)).reshape(group_size, FRAMES, 3, H, HD)
    queries = projected[:, :, 0]
    keys_all = projected[:, :, 1]
    values_all = projected[:, :, 2]
    score_scale = HD ** (-0.5)

    def attend(query_block):
        scores = low_back(jnp.einsum('gqhd,gkhd->ghqk', query_block, keys_all, precision=highest) * score_scale)
        log_total = jax.nn.logsumexp(scores, axis=-1, keepdims=True)
        weights = low(jnp.exp(scores - log_total))
        return jnp.einsum('ghqk,gkhd->gqhd', weights, values_all, precision=highest)
    block_count = FRAMES // QBLOCK
    blocked = queries.reshape(group_size, block_count, QBLOCK, H, HD).transpose(1, 0, 2, 3, 4)
    attended = lax.map(jax.checkpoint(attend), blocked)
    attended = attended.transpose(1, 0, 2, 3, 4).reshape(group_size, FRAMES, D)
    attended = low_back(low(attended))
    branch = low_back(jnp.einsum('gfe,ed->gfd', attended, out_weight, precision=highest) + out_bias)
    hidden = inputs + branch
    act_two = low(layer_norm(hidden, norm2_gain, norm2_bias))
    pre_gelu = low_back(jnp.einsum('gfd,de->gfe', act_two, up_weight, precision=highest) + up_bias)
    act_three = low(jax.nn.gelu(pre_gelu, approximate=False))
    return hidden + jnp.einsum('gfe,ed->gfd', act_three, down_weight, precision=highest) + down_bias

def reference(frames_in, norm1_gain, norm1_bias, qkv_weight, query_bias, value_bias, out_weight, out_bias, norm2_gain, norm2_bias, up_weight, up_bias, down_weight, down_bias, cotangent):
    params = tuple((argument.astype(jnp.float32) for argument in (norm1_gain, norm1_bias, qkv_weight, query_bias, value_bias, out_weight, out_bias, norm2_gain, norm2_bias, up_weight, up_bias, down_weight, down_bias)))
    group_size = math.gcd(CLIPS, 4)
    group_count = CLIPS // group_size
    inputs = frames_in.astype(jnp.float32).reshape(group_count, group_size, FRAMES, D)
    cotangents = cotangent.astype(jnp.float32).reshape(group_count, group_size, FRAMES, D)

    def group_step(running, group_pair):
        group_in, group_cot = group_pair
        output, pullback = jax.vjp(forward, group_in, *params)
        gradients = pullback(group_cot)
        running = tuple((first + second for first, second in zip(running, gradients[1:])))
        return (running, (output.astype(jnp.bfloat16), gradients[0].astype(jnp.bfloat16)))
    zero_totals = tuple((jnp.zeros_like(argument) for argument in params))
    totals, (outputs, in_grads) = lax.scan(group_step, zero_totals, (inputs, cotangents))
    return (outputs.reshape(CLIPS, FRAMES, D), in_grads.reshape(CLIPS, FRAMES, D), totals[0], totals[1], totals[2], totals[3], totals[4], totals[5], totals[6], totals[7], totals[8], totals[9], totals[10], totals[11], totals[12])
```

```python
import jax
import jax.numpy as jnp
from jax import lax
from jax.sharding import PartitionSpec as P

HD = 64
GROUPS = 4
epsilon = 1e-05
BF = jnp.bfloat16
F32 = jnp.float32


def dot(a, b):
    return jnp.dot(a, b, preferred_element_type=F32)


def dot_tn(a, b):
    return lax.dot_general(a, b, (((0,), (0,)), ((), ())), preferred_element_type=F32)


def dot_nt(a, b):
    return lax.dot_general(a, b, (((1,), (1,)), ((), ())), preferred_element_type=F32)


def seq_swap(value, step):
    return lax.ppermute(value, "seq", [(i, i ^ step) for i in range(GROUPS)])


def seq_gather(value):
    near = seq_swap(value, 1)
    far = seq_swap(value, 2)
    cross = seq_swap(far, 1)
    return jnp.concatenate([value, near, far, cross], 0)


def seq_reduce(parts):
    low = parts.astype(BF)
    near = seq_swap(jnp.concatenate([low[1], low[3]], 0), 1).astype(F32)
    rows = parts.shape[1]
    far = seq_swap((parts[2] + near[rows:]).astype(BF), 2).astype(F32)
    return parts[0] + near[:rows] + far


def fsdp_reduce(blocks, count):
    planes = count // 2
    row = lax.axis_index("fsdp")
    plane, side = row // 2, row % 2
    tail = blocks.shape[1:]
    split = blocks.reshape((planes, 2) + tail)
    keep = lax.dynamic_index_in_dim(split, side, 1, keepdims=False)
    give = lax.dynamic_index_in_dim(split, 1 - side, 1, keepdims=False).astype(BF)
    got = lax.ppermute(give, "fsdp", [(i, i ^ 1) for i in range(count)])
    total = keep + got.astype(F32)
    low = total.astype(BF)
    result = lax.dynamic_index_in_dim(total, plane, 0, keepdims=False)
    for step in range(1, planes):
        part = lax.dynamic_index_in_dim(low, plane ^ step, 0, keepdims=False)
        got = lax.ppermute(part, "fsdp", [(i, i ^ (2 * step)) for i in range(count)])
        result = result + got.astype(F32)
    return result


def to_groups(value, count):
    q = count // GROUPS
    pairs = []
    for s in range(GROUPS):
        for j in range(q):
            for t in range(GROUPS):
                pairs.append(((q * s + j) * GROUPS + t, (GROUPS * j + t) * GROUPS + s))
    return lax.ppermute(value, ("fsdp", "seq"), pairs)


def to_owners(value, count):
    q = count // GROUPS
    pairs = []
    for s in range(GROUPS):
        for j in range(q):
            for t in range(GROUPS):
                pairs.append(((GROUPS * j + t) * GROUPS + s, (q * s + j) * GROUPS + t))
    return lax.ppermute(value, ("fsdp", "seq"), pairs)


def normalise(values):
    center = values - jnp.mean(values, -1, keepdims=True)
    rstd = lax.rsqrt(jnp.mean(center * center, -1, keepdims=True) + epsilon)
    return center * rstd, rstd


def norm_back(grad, gain, xhat, rstd):
    e = grad * gain
    return rstd * (
        e - jnp.mean(e, -1, keepdims=True) - xhat * jnp.mean(e * xhat, -1, keepdims=True)
    )


def body(
    frames_in,
    norm1_gain,
    norm1_bias,
    qkv_weight,
    query_bias,
    value_bias,
    out_weight,
    out_bias,
    norm2_gain,
    norm2_bias,
    up_weight,
    up_bias,
    down_weight,
    down_bias,
    cotangent,
):
    count = lax.axis_size("fsdp")
    q = count // GROUPS
    s = lax.axis_index("seq")
    f = lax.axis_index("fsdp")
    width = frames_in.shape[2]
    rows = frames_in.shape[0] * frames_in.shape[1]
    group = width // GROUPS
    heads = group // HD
    own = qkv_weight.shape[0]
    hidden_all = up_weight.shape[1]
    hidden = hidden_all // GROUPS
    hid_own = down_weight.shape[0]

    x = frames_in.reshape(rows, width)
    dy = cotangent.reshape(rows, width)
    x_all = seq_gather(x).astype(F32)

    vectors = jnp.concatenate(
        [
            norm1_gain,
            norm1_bias,
            query_bias,
            value_bias,
            out_bias,
            norm2_gain,
            norm2_bias,
            down_bias,
            up_bias,
        ]
    )
    lines = -(-vectors.shape[0] // (3 * group))
    padded = jnp.pad(vectors, (0, lines * 3 * group - vectors.shape[0])).reshape(lines, 3 * group)
    qkv_own = lax.dynamic_index_in_dim(
        qkv_weight.reshape(own, 3, GROUPS, group), s, 2, keepdims=False
    ).reshape(own, 3 * group)
    first = lax.all_gather(jnp.concatenate([qkv_own, padded], 0), "fsdp", axis=0, tiled=False)
    w_qkv = first[:, :own].reshape(width, 3 * group)
    vec = first[:, own:].reshape(count, lines * 3 * group).astype(F32)
    gain1, bias1, qb, vb, bo, gain2, bias2, bd = (
        vec[:, i * own : (i + 1) * own].reshape(width) for i in range(8)
    )
    bu = vec[:, 8 * own : 8 * own + hid_own].reshape(hidden_all)

    up_own = lax.dynamic_slice_in_dim(up_weight, s * hidden, hidden, 1)
    down_part = lax.dynamic_index_in_dim(
        down_weight.reshape(GROUPS, hid_own // GROUPS, width), s, 0, keepdims=False
    )
    down_part = to_groups(down_part, count)
    second = lax.all_gather(
        jnp.concatenate([up_own, out_weight, down_part], 0), "fsdp", axis=0, tiled=False
    )
    w_up = second[:, :own].reshape(width, hidden)
    w_out = second[:, own : 2 * own].reshape(width, width)
    w_down = second[:, 2 * own :].reshape(hidden, width)

    xhat1, rstd1 = normalise(x_all)
    act1 = (xhat1 * gain1 + bias1).astype(BF)
    bias_qkv = jnp.concatenate(
        [
            lax.dynamic_slice_in_dim(qb, s * group, group),
            jnp.zeros((group,), F32),
            lax.dynamic_slice_in_dim(vb, s * group, group),
        ]
    )
    qkv = (dot(act1, w_qkv) + bias_qkv).astype(BF)
    scale = jnp.asarray(HD ** (-0.5), BF)
    outs, kept = [], []
    for head in range(heads):
        qh = qkv[:, head * HD : (head + 1) * HD] * scale
        kh = qkv[:, group + head * HD : group + (head + 1) * HD]
        vh = qkv[:, 2 * group + head * HD : 2 * group + (head + 1) * HD]
        scores = dot_nt(qh, kh)
        lse = jax.nn.logsumexp(scores, axis=-1, keepdims=True)
        outs.append(dot(jnp.exp(scores - lse).astype(BF), vh).astype(BF))
        kept.append((qh, kh, vh, lse))
    o_own = jnp.concatenate(outs, 1)
    mine = o_own.reshape(GROUPS, rows, group)
    pieces = jnp.stack([mine[0]] + [seq_swap(mine[k], k) for k in range(1, GROUPS)])
    mixed = jnp.concatenate(
        [lax.dynamic_index_in_dim(pieces, p ^ s, 0, keepdims=False) for p in range(GROUPS)], 1
    )

    h = x.astype(F32) + dot(mixed, w_out) + bo
    xhat2, rstd2 = normalise(h)
    act2 = (xhat2 * gain2 + bias2).astype(BF)
    act2_all = seq_gather(act2)
    dy_all = seq_gather(dy)
    u = dot(act2_all, w_up) + lax.dynamic_slice_in_dim(bu, s * hidden, hidden)
    cdf = 0.5 * (1.0 + lax.erf(u * (0.5**0.5)))
    pdf = jnp.exp(-0.5 * u * u) * ((2.0 * jnp.pi) ** (-0.5))
    g = (u * cdf).astype(BF)
    du = (dot_nt(dy_all, w_down) * (cdf + u * pdf)).astype(BF)
    da2 = seq_reduce(dot_nt(du, w_up).reshape(GROUPS, rows, width))
    y = seq_reduce(dot(g, w_down).reshape(GROUPS, rows, width))
    layer_out = (h + y + bd).astype(BF).reshape(frames_in.shape)

    grad_up = fsdp_reduce(dot_tn(act2_all, du).reshape(count, own, hidden), count)
    grad_down = dot_tn(g, dy_all).reshape(q, hid_own, GROUPS, width // GROUPS)
    grad_down = grad_down.transpose(0, 2, 1, 3).reshape(count, hid_own, width // GROUPS)
    grad_down = to_owners(fsdp_reduce(grad_down, count).astype(BF), count).astype(F32)

    dh = dy.astype(F32) + norm_back(da2, gain2, xhat2, rstd2)
    db = dh.astype(BF)
    d_mixed = dot_nt(db, w_out).astype(BF).reshape(rows, GROUPS, group)
    pieces = [lax.dynamic_index_in_dim(d_mixed, s ^ k, 1, keepdims=False) for k in range(GROUPS)]
    d_heads = jnp.concatenate(
        [pieces[0]] + [seq_swap(pieces[k], k) for k in range(1, GROUPS)], 0
    )
    db_all = seq_gather(db)
    grad_out = dot_tn(o_own, db_all).reshape(q, own, GROUPS, width // GROUPS)
    grad_out = grad_out.transpose(0, 2, 1, 3).reshape(count, own, width // GROUPS)
    grad_out = to_owners(fsdp_reduce(grad_out, count).astype(BF), count).astype(F32)

    dqs, dks, dvs = [], [], []
    for head in range(heads):
        qh, kh, vh, lse = kept[head]
        doh = d_heads[:, head * HD : (head + 1) * HD]
        probs = jnp.exp(dot_nt(qh, kh) - lse)
        dvs.append(dot_tn(probs.astype(BF), doh).astype(BF))
        dp = dot_nt(doh, vh)
        ds = (probs * (dp - jnp.sum(probs * dp, -1, keepdims=True))).astype(BF)
        dqs.append((dot(ds, kh) * HD ** (-0.5)).astype(BF))
        dks.append(dot_tn(ds, qh).astype(BF))
    dqkv = jnp.concatenate(dqs + dks + dvs, 1)

    grad_qkv = fsdp_reduce(dot_tn(act1, dqkv).reshape(count, own, 3 * group), count)
    units = grad_qkv.astype(BF).reshape(own, 3, group)
    order = jnp.array([[0, 1, 2], [1, 0, 2], [1, 2, 0], [2, 1, 0]], jnp.int32)[s]
    got = [
        lax.dynamic_index_in_dim(units, order[k], 1, keepdims=False) for k in range(3)
    ]
    got = [got[0], seq_swap(got[1], 1), seq_swap(got[2], 2)]
    odd = s % 2 == 1
    grad_qkv = jnp.concatenate(
        [jnp.where(odd, got[2], got[0]), got[1], jnp.where(odd, got[0], got[2])], 1
    ).astype(F32)

    da1 = dot_nt(dqkv, w_qkv)
    d1 = seq_reduce(da1.reshape(GROUPS, rows, width))
    input_grad = (
        (dh + norm_back(d1, gain1, xhat1[:rows], rstd1[:rows])).astype(BF).reshape(frames_in.shape)
    )

    def placed(values, size):
        return lax.dynamic_update_slice_in_dim(
            jnp.zeros((size,), F32), values, s * values.shape[0], 0
        )

    early = lax.psum(
        jnp.concatenate(
            [
                jnp.sum(db.astype(F32), 0),
                jnp.sum(da2 * xhat2, 0),
                jnp.sum(da2, 0),
                jnp.sum(dy.astype(F32), 0),
                placed(jnp.sum(du.astype(F32), 0), hidden_all),
            ]
        ),
        ("fsdp", "seq"),
    )
    dsum = jnp.sum(dqkv.astype(F32), 0)
    late = lax.psum(
        jnp.concatenate(
            [
                jnp.sum(da1 * xhat1, 0),
                jnp.sum(da1, 0),
                placed(dsum[:group], width),
                placed(dsum[2 * group :], width),
            ]
        ),
        ("fsdp", "seq"),
    )

    def mine_of(total, index, size):
        return lax.dynamic_slice_in_dim(total, index * width + f * size, size)

    return (
        layer_out,
        input_grad,
        mine_of(late, 0, own),
        mine_of(late, 1, own),
        grad_qkv,
        mine_of(late, 2, own),
        mine_of(late, 3, own),
        grad_out,
        mine_of(early, 0, own),
        mine_of(early, 1, own),
        mine_of(early, 2, own),
        grad_up,
        mine_of(early, 4, hid_own),
        grad_down,
        mine_of(early, 3, own),
    )


def solution(mesh):
    tokens = P("fsdp", "seq", None)
    vector = P("fsdp")
    matrix = P("fsdp", None)
    summed = P("fsdp", "seq")
    return jax.shard_map(
        body,
        mesh=mesh,
        in_specs=(
            tokens,
            vector,
            vector,
            matrix,
            vector,
            vector,
            matrix,
            vector,
            vector,
            vector,
            matrix,
            vector,
            matrix,
            vector,
            tokens,
        ),
        out_specs=(
            tokens,
            tokens,
            vector,
            vector,
            summed,
            vector,
            vector,
            summed,
            vector,
            vector,
            vector,
            summed,
            vector,
            summed,
            vector,
        ),
        check_vma=False,
    )
```

```python
import functools

import jax
import jax.numpy as jnp
from jax import lax
from jax.experimental import pallas as pl
from jax.experimental.pallas import tpu as pltpu
from jax.sharding import PartitionSpec as P

HD = 64
GROUPS = 4
epsilon = 1e-05
BF = jnp.bfloat16
F32 = jnp.float32


def dot(a, b):
    return jnp.dot(a, b, preferred_element_type=F32)


def dot_tn(a, b):
    return lax.dot_general(a, b, (((0,), (0,)), ((), ())), preferred_element_type=F32)


def dot_nt(a, b):
    return lax.dot_general(a, b, (((1,), (1,)), ((), ())), preferred_element_type=F32)


def seq_swap(value, step):
    return lax.ppermute(value, "seq", [(i, i ^ step) for i in range(GROUPS)])


def seq_pieces(value):
    near = seq_swap(value, 1)
    far = seq_swap(value, 2)
    return [value, near, far, seq_swap(far, 1)]


def fsdp_reduce(blocks):
    return lax.psum_scatter(blocks, "fsdp", scatter_dimension=0, tiled=False)


def side_swap(value, count):
    return lax.ppermute(value, "fsdp", [(i, i ^ 1) for i in range(count)])


def plane_swaps(parts, count):
    return [
        lax.ppermute(part, "fsdp", [(i, i ^ (2 * step)) for i in range(count)])
        for step, part in enumerate(parts, 1)
    ]


def add_all(own, arrived):
    for part in arrived:
        own = own + part.astype(F32)
    return own


def ring_order(count):
    return list(range(0, count, 2)) + list(range(count - 1, 0, -2))


def ring_gather(value, count):
    order = ring_order(count)
    ahead = [(order[i], order[(i + 1) % count]) for i in range(count)]
    back = [(b, a) for a, b in ahead]
    blocks, shifts = [value], [0]
    left = right = value
    for step in range(1, count // 2 + 1):
        left = lax.ppermute(left, "fsdp", ahead)
        blocks.append(left)
        shifts.append(-step)
        if step < count // 2:
            right = lax.ppermute(right, "fsdp", back)
            blocks.append(right)
            shifts.append(step)
    spot = jnp.array([order.index(i) for i in range(count)], jnp.int32)[lax.axis_index("fsdp")]
    sources = jnp.array(order, jnp.int32)[(spot + jnp.array(shifts, jnp.int32)) % count]
    return sources, blocks


def after(value, *others):
    return lax.optimization_barrier((value,) + others)[0]


def to_groups(value, count):
    q = count // GROUPS
    pairs = []
    for s in range(GROUPS):
        for j in range(q):
            for t in range(GROUPS):
                pairs.append(((q * s + j) * GROUPS + t, (GROUPS * j + t) * GROUPS + s))
    return lax.ppermute(value, ("fsdp", "seq"), pairs)


def to_owners(value, count, step):
    q = count // GROUPS
    pairs = []
    for s in range(GROUPS):
        for j in range(q):
            for t in range(GROUPS):
                pairs.append(
                    ((GROUPS * j + t) * GROUPS + s, (q * s + j) * GROUPS + (t ^ step))
                )
    return lax.ppermute(value, ("fsdp", "seq"), pairs)


def normalise(values):
    center = values - jnp.mean(values, -1, keepdims=True)
    rstd = lax.rsqrt(jnp.mean(center * center, -1, keepdims=True) + epsilon)
    return center * rstd, rstd


def norm_back(grad, gain, xhat, rstd):
    e = grad * gain
    return rstd * (
        e - jnp.mean(e, -1, keepdims=True) - xhat * jnp.mean(e * xhat, -1, keepdims=True)
    )


def params(megabytes=26):
    return pltpu.CompilerParams(vmem_limit_bytes=megabytes * 2**20)


def cost(flops, moved, exps=0):
    return pl.CostEstimate(flops=flops, bytes_accessed=moved, transcendentals=exps)


SMEM = pl.BlockSpec(memory_space=pltpu.SMEM)
VMEM = pl.BlockSpec(memory_space=pltpu.VMEM)
ANY = pl.BlockSpec(memory_space=pl.ANY)


def run(kernel, scalars, arrays, out_shape, scratch, estimate, megabytes=28):
    n_scalars, n_arrays, n_outs = len(scalars), len(arrays), len(out_shape)

    def wrapped(*refs):
        rest = refs[n_scalars + n_arrays :]
        outs, own = rest[:n_outs], rest[n_outs : n_outs + len(scratch)]
        held, sems = rest[n_outs + len(scratch) : -1], rest[-1]
        copies = [
            pltpu.make_async_copy(refs[n_scalars + i], held[i], sems.at[i])
            for i in range(n_arrays)
        ]
        for copy in copies:
            copy.start()
        for copy in copies:
            copy.wait()
        kernel(*refs[:n_scalars], *held, *outs, *own)

    return pl.pallas_call(
        wrapped,
        out_shape=tuple(out_shape),
        in_specs=[SMEM] * n_scalars + [ANY] * n_arrays,
        out_specs=(VMEM,) * n_outs,
        scratch_shapes=list(scratch)
        + [pltpu.VMEM(a.shape, a.dtype) for a in arrays]
        + [pltpu.SemaphoreType.DMA((n_arrays,))],
        compiler_params=params(megabytes),
        cost_estimate=estimate,
    )(*scalars, *arrays)


def assemble(where, blocks, out, rows):
    if len(blocks) == 1:
        out[...] = blocks[0][...]
        return
    for i, block in enumerate(blocks):
        start = pl.multiple_of(where[i] * rows, rows)
        out[pl.ds(start, rows), :] = block[:rows, :]


def lane_ids(width):
    return lax.broadcasted_iota(jnp.int32, (1, width), 1)


def collect_vectors(where, me, blocks, own, group, vec, table):
    count = len(blocks)
    width = count * own
    table[...] = jnp.zeros_like(table)
    for i, block in enumerate(blocks):
        pair = block[own : own + 2, :].astype(F32)
        table[0, pl.ds(where[i], 1), :] = pair[0:1]
        table[1, pl.ds(where[i], 1), :] = pair[1:2]
    lanes = lax.broadcasted_iota(jnp.int32, (count, width), 1)
    rows = lax.broadcasted_iota(jnp.int32, (count, width), 0)
    mine = (lanes >= rows * own) & (lanes < (rows + 1) * own)
    base = table[0]
    shifted = [base] + [pltpu.roll(base, k * own, 1) for k in range(1, count)]

    def whole(index):
        picked = jnp.zeros((count, width), F32)
        for k in range(count):
            here = mine & (rows == (k + index) % count)
            picked = jnp.where(here, shifted[k], picked)
        return jnp.sum(picked, 0, keepdims=True)

    gain1, bias1, qb, vb, bo, gain2, bias2, bd = (whole(i) for i in range(8))
    lane = lane_ids(width)
    qb = pltpu.roll(qb, lax.rem(width - me * group, width), 1)
    vb = pltpu.roll(vb, lax.rem(width + 2 * group - me * group, width), 1)
    bias = jnp.where(lane < group, qb, 0.0)
    bias = jnp.where((lane >= 2 * group) & (lane < 3 * group), vb, bias)
    first = table[1, pl.ds(2 * me, 1), :]
    second = pltpu.roll(table[1, pl.ds(2 * me + 1, 1), :], width // 2, 1)
    bu = jnp.where(lane < width // 2, first, second)
    for i, row in enumerate((gain1, bias1, bias, bo, gain2, bias2, bd, bu)):
        vec[i : i + 1, :] = row


def project_kernel(ring, own, group, rows, *refs):
    where, place_ref = refs[0], refs[1]
    x_refs = refs[2:6]
    n_blocks = 8 if ring else 1
    blocks = refs[6 : 6 + n_blocks]
    rest = refs[6 + n_blocks :]
    if not ring:
        vec_in, rest = rest[0], rest[1:]
    act, queries, keys, values, k_turned, v_turned, w, w_col, vec, table = rest
    me = place_ref[0]
    heads = group // HD
    if ring:
        collect_vectors(where, me, blocks, own, group, vec, table)
    else:
        vec[...] = vec_in[...]
    if ring:
        for i, block in enumerate(blocks):
            start = pl.multiple_of(where[i] * own, own)
            w[pl.ds(start, own), :] = block[:own, : 3 * group]
            w_col[pl.ds(start, own), :] = block[:own, 3 * group :]
    else:
        w[...] = blocks[0][...]
        w_col[...] = jnp.zeros_like(w_col)
    gain, shift, bias = vec[0:1, :], vec[1:2, :], vec[2:3, : 3 * group]
    for k in range(4):
        here = slice(k * rows, (k + 1) * rows)
        xhat, _ = normalise(x_refs[k][...].astype(F32))
        block = (xhat * gain + shift).astype(BF)
        act[here, :] = block
        qkv = (dot(block, w[...]) + bias).astype(BF)
        queries[here, :] = qkv[:, :group] * jnp.asarray(HD ** (-0.5), BF)
        for head in range(heads):
            keys[head, here, :] = qkv[:, group + head * HD : group + (head + 1) * HD]
            values[head, here, :] = qkv[:, 2 * group + head * HD : 2 * group + (head + 1) * HD]
        k_turned[:, here] = qkv[:, group : 2 * group].T
        v_turned[:, here] = qkv[:, 2 * group : 3 * group].T


def project(where, me, pieces, blocks, vec, own, group):
    rows, width = pieces[0].shape
    frames = 4 * rows
    heads = group // HD
    ring = len(blocks) > 1
    out_shape = (
        jax.ShapeDtypeStruct((frames, width), BF),
        jax.ShapeDtypeStruct((frames, group), BF),
        jax.ShapeDtypeStruct((heads, frames, HD), BF),
        jax.ShapeDtypeStruct((heads, frames, HD), BF),
        jax.ShapeDtypeStruct((group, frames), BF),
        jax.ShapeDtypeStruct((group, frames), BF),
        jax.ShapeDtypeStruct((width, 3 * group), BF),
        jax.ShapeDtypeStruct((width, group), BF),
        jax.ShapeDtypeStruct((8, width), F32),
    )
    args = [where, me, *pieces, *blocks] + ([] if ring else [vec])
    return run(
        functools.partial(project_kernel, ring, own, group, rows),
        args[:2],
        args[2:],
        out_shape,
        [pltpu.VMEM((2, 8, width), F32)],
        cost(5 * 10**9, 8 * 10**6),
    )


def attend_kernel(group, rows, part, queries, keys, v_turned, first, second, lse):
    heads = group // HD
    lse[...] = jnp.zeros_like(lse)
    for t, out in enumerate((first, second)):
        turned = []
        for head in range(heads):
            start = (2 * part + t) * rows
            query = queries[start : start + rows, head * HD : (head + 1) * HD]
            scores = dot_nt(keys[head], query)
            top = jnp.max(scores, 0, keepdims=True)
            e = jnp.exp(scores - top)
            total = jnp.sum(e, 0, keepdims=True)
            lse[head : head + 1, t * rows : (t + 1) * rows] = top + jnp.log(total)
            p = (e * (1.0 / total)).astype(BF)
            turned.append(dot(v_turned[head * HD : (head + 1) * HD, :], p))
        out[...] = jnp.concatenate(turned, 0).T.astype(BF)


def attend(part, queries, keys, v_turned):
    frames, group = queries.shape
    rows = frames // 4
    return run(
        functools.partial(attend_kernel, group, rows, part),
        [],
        [queries, keys, v_turned],
        (
            jax.ShapeDtypeStruct((rows, group), BF),
            jax.ShapeDtypeStruct((rows, group), BF),
            jax.ShapeDtypeStruct((8, 2 * rows), F32),
        ),
        [],
        cost(5 * 10**9, 2 * 10**6, 3 * 2**19),
    )


def mix_kernel(own, group, rows, *refs):
    where, place_ref, vec, x = refs[:4]
    o_refs = refs[4:8]
    blocks, (h, act, w) = refs[8:-3], refs[-3:]
    me = place_ref[0]
    if len(blocks) == 1:
        w[...] = blocks[0][...]
    else:
        for k, block in enumerate(blocks):
            for c in range(4):

                @pl.when((me ^ k) == c)
                def _(block=block, c=c):
                    w[:, c * group : (c + 1) * group] = block[...]

    total = x[...].astype(F32) + vec[3:4, :]
    for k in range(4):
        start = pl.multiple_of((me ^ k) * group, group)
        total = total + dot(o_refs[k][:rows, :], w[pl.ds(start, group), :])
    h[...] = total
    xhat, _ = normalise(total)
    act[...] = (xhat * vec[4:5, :] + vec[5:6, :]).astype(BF)


def mix(where, me, vec, x, pieces, blocks, own, group):
    rows, width = x.shape
    args = [where, me, vec, x, *pieces, *blocks]
    return run(
        functools.partial(mix_kernel, own, group, rows),
        args[:2],
        args[2:],
        (
            jax.ShapeDtypeStruct((rows, width), F32),
            jax.ShapeDtypeStruct((rows, width), BF),
            jax.ShapeDtypeStruct((width, width), BF),
        ),
        [],
        cost(3 * 10**8, 4 * 10**6),
    )


def feed_kernel(n_up, n_down, own, rows, *refs):
    where, vec, a0, a1, dy0, dy1 = refs[:6]
    ups = refs[6 : 6 + n_up]
    downs = refs[6 + n_up : 6 + n_up + n_down]
    g, du, first, second, total, w_up, w_down = refs[6 + n_up + n_down :]
    if n_down:
        w_up[...] = ups[0][...]
        w_down[...] = downs[0][...]
    else:
        assemble(where, ups, w_up, own)
        for i, block in enumerate(ups):
            start = pl.multiple_of(where[i] * own, own)
            w_down[pl.ds(start, own), :] = block[own : 2 * own, :]
    bias = vec[7:8, :]
    total[...] = jnp.zeros_like(total)
    chunk = rows // 2
    for part, (a, dy, out) in enumerate(((a0, dy0, first), (a1, dy1, second))):
        for c in range(2):
            here = slice(c * chunk, (c + 1) * chunk)
            there = slice(part * rows + c * chunk, part * rows + (c + 1) * chunk)
            u = dot(a[here, :], w_up[...]) + bias
            cdf = 0.5 * (1.0 + lax.erf(u * (0.5**0.5)))
            pdf = jnp.exp(-0.5 * u * u) * ((2.0 * jnp.pi) ** (-0.5))
            g[there, :] = (u * cdf).astype(BF)
            grad = (dot_nt(dy[here, :], w_down[...]) * (cdf + u * pdf)).astype(BF)
            du[there, :] = grad
            total[0:1, :] += jnp.sum(grad.astype(F32), 0, keepdims=True)
            out[here, :] = dot_nt(grad, w_up[...]).astype(out.dtype)


def feed(where, vec, acts, dys, ups, downs, own):
    rows, width = acts[0].shape
    hidden = ups[0].shape[1]
    args = [where, vec, *acts, *dys, *ups, *downs]
    return run(
        functools.partial(feed_kernel, len(ups), len(downs), own, rows),
        args[:1],
        args[1:],
        (
            jax.ShapeDtypeStruct((2 * rows, hidden), BF),
            jax.ShapeDtypeStruct((2 * rows, hidden), BF),
            jax.ShapeDtypeStruct((rows, width), F32),
            jax.ShapeDtypeStruct((rows, width), BF),
            jax.ShapeDtypeStruct((8, hidden), F32),
            jax.ShapeDtypeStruct((width, hidden), BF),
            jax.ShapeDtypeStruct((hidden, width), BF),
        ),
        [],
        cost(18 * 10**8, 8 * 10**6, 2**19),
    )


def feed_out_kernel(rows, g_a, g_b, w, first, third, sent):
    for k in (1, 3, 0, 2):
        here = slice((k % 2) * rows, (k % 2 + 1) * rows)
        part = dot((g_a if k < 2 else g_b)[here, :], w[...])
        if k == 0:
            first[...] = part
        elif k == 2:
            third[...] = part
        else:
            sent[(k // 2) * rows : (k // 2 + 1) * rows, :] = part.astype(BF)


def feed_out(gs, w):
    rows = gs[0].shape[0] // 2
    width = w.shape[1]
    return run(
        functools.partial(feed_out_kernel, rows),
        [],
        [*gs, w],
        (
            jax.ShapeDtypeStruct((rows, width), F32),
            jax.ShapeDtypeStruct((rows, width), F32),
            jax.ShapeDtypeStruct((2 * rows, width), BF),
        ),
        [],
        cost(12 * 10**8, 5 * 10**6),
    )


def turn_kernel(group, rows, *refs):
    place_ref, vec, h, dy, part, near, far, w = refs[:8]
    dh, db, d0, d1, d2, d3, sums = refs[8:]
    me = place_ref[0]
    da = part[...] + near[...].astype(F32) + far[...].astype(F32)
    xhat, rstd = normalise(h[...])
    cot = dy[...].astype(F32)
    grad = cot + norm_back(da, vec[4:5, :], xhat, rstd)
    dh[...] = grad
    low = grad.astype(BF)
    db[...] = low
    for k, out in enumerate((d0, d1, d2, d3)):
        start = pl.multiple_of((me ^ k) * group, group)
        out[...] = dot_nt(low, w[pl.ds(start, group), :]).astype(BF)
    sums[...] = jnp.zeros_like(sums)
    sums[0:1, :] = jnp.sum(low.astype(F32), 0, keepdims=True)
    sums[1:2, :] = jnp.sum(da * xhat, 0, keepdims=True)
    sums[2:3, :] = jnp.sum(da, 0, keepdims=True)
    sums[3:4, :] = jnp.sum(cot, 0, keepdims=True)


def turn(me, vec, h, dy, part, near, far, w, group):
    rows, width = h.shape
    piece = jax.ShapeDtypeStruct((rows, group), BF)
    return run(
        functools.partial(turn_kernel, group, rows),
        [me],
        [vec, h, dy, part, near, far, w],
        (
            jax.ShapeDtypeStruct((rows, width), F32),
            jax.ShapeDtypeStruct((rows, width), BF),
            piece,
            piece,
            piece,
            piece,
            jax.ShapeDtypeStruct((8, width), F32),
        ),
        [],
        cost(3 * 10**8, 5 * 10**6),
    )


def owner_rows(grads, keep, give, side, own):
    for z in range(keep.shape[0]):
        keep[z] = grads[pl.ds(pl.multiple_of((2 * z + side) * own, own), own), :]
        rest = grads[pl.ds(pl.multiple_of((2 * z + 1 - side) * own, own), own), :]
        give[z] = rest.astype(BF)


def back_tiles(group, rows, part, queries, keys, values, k_turned, lse, d_refs, dk, dv, dq, skip):
    heads = group // HD
    for t in range(2):
        start = (2 * part + t) * rows
        turned = []
        for head in range(heads):
            here = slice(head * HD, (head + 1) * HD)
            query = queries[start : start + rows, here]
            d_out = d_refs[t][:, here]
            scores = dot_nt(keys[head], query)
            p = jnp.exp(scores - lse[head : head + 1, t * rows : (t + 1) * rows])
            dv[head] += dot(p.astype(BF), d_out)
            dp = dot_nt(values[head], d_out)
            inner = jnp.sum(p * dp, 0, keepdims=True)
            ds = (p * (dp - inner)).astype(BF)
            dk[head] += dot(ds, query)
            turned.append(dot(k_turned[here, :], ds))
        dq[skip + t * rows : skip + (t + 1) * rows, :group] = (
            jnp.concatenate(turned, 0).T * HD ** (-0.5)
        ).astype(BF)


def back_first_kernel(group, rows, queries, keys, values, k_turned, lse, d0, d1, dq, dk, dv):
    dk[...] = jnp.zeros_like(dk)
    dv[...] = jnp.zeros_like(dv)
    back_tiles(group, rows, 0, queries, keys, values, k_turned, lse, (d0, d1), dk, dv, dq, 0)


def back_first(queries, keys, values, k_turned, lse, d0, d1):
    frames, group = queries.shape
    heads = group // HD
    total = jax.ShapeDtypeStruct((heads, frames, HD), F32)
    return run(
        functools.partial(back_first_kernel, group, frames // 4),
        [],
        [queries, keys, values, k_turned, lse, d0, d1],
        (jax.ShapeDtypeStruct((frames // 2, group), BF), total, total),
        [],
        cost(10 * 10**9, 4 * 10**6, 3 * 2**19),
    )


def back_second_kernel(own, group, rows, split, *refs):
    place_ref, queries, keys, values, k_turned, lse, d2, d3 = refs[:8]
    dq_first, dk_first, dv_first, act = refs[8:12]
    if split:
        o_refs, db_refs = refs[12:16], refs[16:20]
        dqkv, keep, give, dk, dv, grads = refs[20:]
    else:
        dqkv, grads, dk, dv = refs[12:]
    heads = group // HD
    dk[...] = dk_first[...]
    dv[...] = dv_first[...]
    dqkv[: 2 * rows, :group] = dq_first[...]
    d_refs = (d2, d3)
    back_tiles(group, rows, 1, queries, keys, values, k_turned, lse, d_refs, dk, dv, dqkv, 2 * rows)
    dqkv[:, group : 2 * group] = jnp.concatenate([dk[i] for i in range(heads)], 1).astype(BF)
    dqkv[:, 2 * group :] = jnp.concatenate([dv[i] for i in range(heads)], 1).astype(BF)
    if split:
        out = 0.0
        for k in range(4):
            out = out + dot_tn(o_refs[k][...], db_refs[k][...])
        for j in range(2):
            for t in range(4):
                start = (j * 4 + t) * own
                grads[start : start + own, 3 * group :] = out[
                    j * own : (j + 1) * own, t * group : (t + 1) * group
                ]
        grads[:, : 3 * group] = dot_tn(act[...], dqkv[...])
        owner_rows(grads, keep, give, place_ref[1], own)
    else:
        grads[...] = dot_tn(act[...], dqkv[...])


def back_second(me, queries, keys, values, k_turned, lse, ds, first, act, os, dbs, own, planes):
    frames, group = queries.shape
    heads = group // HD
    width = act.shape[1]
    split = planes > 1
    out_shape = [jax.ShapeDtypeStruct((frames, 3 * group), BF)]
    scratch = [
        pltpu.VMEM((heads, frames, HD), F32),
        pltpu.VMEM((heads, frames, HD), F32),
    ]
    if split:
        out_shape.append(jax.ShapeDtypeStruct((planes, own, width), F32))
        out_shape.append(jax.ShapeDtypeStruct((planes, own, width), BF))
        scratch.append(pltpu.VMEM((width, width), F32))
    else:
        out_shape.append(jax.ShapeDtypeStruct((width, 3 * group), F32))
    return run(
        functools.partial(back_second_kernel, own, group, frames // 4, split),
        [me],
        [queries, keys, values, k_turned, lse, *ds, *first, act] + ([*os, *dbs] if split else []),
        tuple(out_shape),
        scratch,
        cost(12 * 10**9, 6 * 10**6, 3 * 2**19),
    )


def feed_grads_kernel(own, rows, split, *refs):
    place_ref = refs[0]
    acts, dys = refs[1:5], refs[5:9]
    g_a, g_b, du_a, du_b = refs[9:13]
    if split:
        up_keep, up_give, down_keep, down_give, grads = refs[13:]
    else:
        up, down = refs[13:]
    for turn_of in range(2):
        if split:
            out = grads
        else:
            out = up if turn_of == 0 else down
        total = 0.0
        for k in range(4):
            here = slice((k % 2) * rows, (k % 2 + 1) * rows)
            if turn_of == 0:
                total = total + dot_tn(acts[k][...], (du_a if k < 2 else du_b)[here, :])
            else:
                total = total + dot_tn((g_a if k < 2 else g_b)[here, :], dys[k][...])
        out[...] = total
        if split:
            if turn_of == 0:
                owner_rows(grads, up_keep, up_give, place_ref[1], own)
            else:
                owner_rows(grads, down_keep, down_give, place_ref[1], own)


def feed_grads(me, acts, dys, gs, dus, own, planes):
    rows, width = acts[0].shape
    hidden = gs[0].shape[1]
    split = planes > 1
    if split:
        keep = jax.ShapeDtypeStruct((planes, own, hidden), F32)
        give = jax.ShapeDtypeStruct((planes, own, hidden), BF)
        out_shape = (keep, give, keep, give)
        scratch = [pltpu.VMEM((width, hidden), F32)]
    else:
        out_shape = (jax.ShapeDtypeStruct((width, hidden), F32),) * 2
        scratch = []
    return run(
        functools.partial(feed_grads_kernel, own, rows, split),
        [me],
        [*acts, *dys, *gs, *dus],
        out_shape,
        scratch,
        cost(24 * 10**8, 16 * 10**6),
    )


def out_grads_kernel(own, group, *refs):
    o_refs, db_refs, blocks = refs[1:5], refs[5:9], refs[9]
    total = 0.0
    for k in range(4):
        total = total + dot_tn(o_refs[k][...], db_refs[k][...])
    for j in range(group // own):
        for t in range(4):
            blocks[j * 4 + t] = total[j * own : (j + 1) * own, t * group : (t + 1) * group]


def out_grads(me, os, dbs, own):
    group = os[0].shape[1]
    return run(
        functools.partial(out_grads_kernel, own, group),
        [me],
        [*os, *dbs],
        (jax.ShapeDtypeStruct((group // own * 4, own, group), F32),),
        [],
        cost(3 * 10**8, 5 * 10**6),
    )


def plane_kernel(number, *refs):
    place_ref = refs[0]
    plane = place_ref[2]
    for i in range(number):
        keep, got = refs[1 + 2 * i], refs[2 + 2 * i]
        outs = refs[1 + 2 * number + i * keep.shape[0] :]
        for step in range(keep.shape[0]):
            total = keep[plane ^ step] + got[plane ^ step].astype(F32)
            outs[step][...] = total.astype(outs[step].dtype)


def plane_parts(me, pairs):
    args, out_shape = [], []
    for keep, got in pairs:
        args += [keep, got]
        for step in range(keep.shape[0]):
            out_shape.append(jax.ShapeDtypeStruct(keep.shape[1:], F32 if step == 0 else BF))
    outs = run(
        functools.partial(plane_kernel, len(pairs)),
        [me],
        [*args],
        tuple(out_shape),
        [],
        cost(10**6, 6 * 10**6),
    )
    size = len(outs) // len(pairs)
    return [outs[i * size : (i + 1) * size] for i in range(len(pairs))]


def project_back_kernel(rows, place_ref, dqkv, w, *refs):
    x_refs = refs[:4]
    first, third, sent1, sent3, sums = refs[4:]
    group = dqkv.shape[1] // 3
    gain_sum, shift_sum = 0.0, 0.0
    for k in (1, 3, 0, 2):
        part = dot_nt(dqkv[k * rows : (k + 1) * rows, :], w[...])
        xhat, _ = normalise(x_refs[k][...].astype(F32))
        gain_sum = gain_sum + jnp.sum(part * xhat, 0, keepdims=True)
        shift_sum = shift_sum + jnp.sum(part, 0, keepdims=True)
        if k == 0:
            first[...] = part
        elif k == 2:
            third[...] = part
        else:
            (sent1 if k == 1 else sent3)[...] = part.astype(BF)
    sums[...] = jnp.zeros_like(sums)
    sums[0:1, :] = gain_sum
    sums[1:2, :] = shift_sum
    sums[2:3, : 3 * group] = jnp.sum(dqkv[...].astype(F32), 0, keepdims=True)


def project_back(me, dqkv, w, pieces):
    rows, width = pieces[0].shape
    return run(
        functools.partial(project_back_kernel, rows),
        [me],
        [dqkv, w, *pieces],
        (
            jax.ShapeDtypeStruct((rows, width), F32),
            jax.ShapeDtypeStruct((rows, width), F32),
            jax.ShapeDtypeStruct((rows, width), BF),
            jax.ShapeDtypeStruct((rows, width), BF),
            jax.ShapeDtypeStruct((8, width), F32),
        ),
        [],
        cost(9 * 10**8, 8 * 10**6),
    )


def finish_kernel(vec, x, dh, part, near, far, out):
    da = part[...] + near[...].astype(F32) + far[...].astype(F32)
    xhat, rstd = normalise(x[...].astype(F32))
    out[...] = (dh[...] + norm_back(da, vec[0:1, :], xhat, rstd)).astype(BF)


def finish(vec, x, dh, part, near, far):
    return run(
        finish_kernel,
        [],
        [vec, x, dh, part, near, far],
        (jax.ShapeDtypeStruct(x.shape, BF),),
        [],
        cost(10**7, 4 * 10**6),
    )[0]


def pack_kernel(own, place_ref, sums1, sums2, usum_a, usum_b, keep, give, table, lines):
    me, side = place_ref[0], place_ref[1]
    width = sums1.shape[1]
    group = width // 4
    count = width // own
    lane = lane_ids(width)
    dsum = sums1[2:3, :]
    query = jnp.where(lane < group, dsum, 0.0)
    value = jnp.where(lane < group, pltpu.roll(dsum, 2 * group, 1), 0.0)
    table[0:2, :] = sums1[0:2, :]
    table[2:3, :] = pltpu.roll(query, me * group, 1)
    table[3:4, :] = pltpu.roll(value, me * group, 1)
    table[4:8, :] = sums2[0:4, :]
    base = table[...]
    shifted = [base] + [pltpu.roll(base, k * own, 1) for k in range(1, count)]
    lanes = lax.broadcasted_iota(jnp.int32, (count, width), 1)
    rows = lax.broadcasted_iota(jnp.int32, (count, width), 0)
    mine = (lanes >= rows * own) & (lanes < (rows + 1) * own)
    lines[...] = jnp.zeros_like(lines)
    for f in range(count):
        picked = jnp.zeros((count, width), F32)
        for k in range(count):
            picked = jnp.where(mine & (rows == (f + k) % count), shifted[k], picked)
        lines[f : f + 1, :width] = jnp.sum(picked, 0, keepdims=True)
    total = usum_a[0:1, :] + usum_b[0:1, :]
    half = width // 2
    lines[pl.ds(2 * me, 1), width:] = total[:, :half]
    lines[pl.ds(2 * me + 1, 1), width:] = total[:, half:]
    for z in range(count // 2):
        keep[z : z + 1, :] = lines[pl.ds(2 * z + side, 1), :]
        give[z : z + 1, :] = lines[pl.ds(2 * z + 1 - side, 1), :]


def pack(me, sums1, sums2, usum_a, usum_b, own):
    width = sums1.shape[1]
    wide = width + width // 2
    count = width // own
    return run(
        functools.partial(pack_kernel, own),
        [me],
        [sums1, sums2, usum_a, usum_b],
        (jax.ShapeDtypeStruct((count // 2, wide), F32),) * 2,
        [pltpu.VMEM((8, width), F32), pltpu.VMEM((count, wide), F32)],
        cost(10**6, 10**5),
    )


def unpack_kernel(own, place_ref, own_sum, got1, got2, got3, *outs):
    me = place_ref[0]
    total = own_sum[...]
    for got in (got1, got2, got3):
        total = total + got[...].astype(F32)
    low = total.astype(BF)
    group = low.shape[1] // 4
    orders = ((0, 1, 2), (1, 0, 2), (1, 2, 0), (2, 1, 0))
    for s in range(4):

        @pl.when(me == s)
        def _(s=s):
            for k in range(3):
                unit = orders[s][k]
                outs[k][...] = low[:, unit * group : (unit + 1) * group]

    outs[3][...] = low[:, 3 * group :]


def unpack(me, own_sum, arrived):
    own, width = own_sum.shape
    return run(
        functools.partial(unpack_kernel, own),
        [me],
        [own_sum, *arrived],
        (jax.ShapeDtypeStruct((own, width // 4), BF),) * 4,
        [],
        cost(10**6, 10**6),
    )


def feed_sums_kernel(place_ref, up, up1, up2, up3, down, down1, down2, down3, *outs):
    spot = place_ref[3]
    up_out = outs[0]
    up_out[...] = up[...] + up1[...].astype(F32) + up2[...].astype(F32) + up3[...].astype(F32)
    total = down[...]
    for got in (down1, down2, down3):
        total = total + got[...].astype(F32)
    low = total.astype(BF)
    group = low.shape[1] // 4
    for t in range(4):

        @pl.when(spot == t)
        def _(t=t):
            for k in range(4):
                c = t ^ k
                outs[1 + k][...] = low[:, c * group : (c + 1) * group]


def feed_sums(me, up, ups, down, downs):
    own, width = down.shape
    return run(
        feed_sums_kernel,
        [me],
        [up, *ups, down, *downs],
        (jax.ShapeDtypeStruct(up.shape, F32),)
        + (jax.ShapeDtypeStruct((own, width // 4), BF),) * 4,
        [],
        cost(10**6, 3 * 10**6),
    )


def settle_kernel(place_ref, d0, d1, d2, d3, out, down_grad, out_grad):
    me = place_ref[0]
    own = d0.shape[0]
    for k, piece in enumerate((d0, d1, d2, d3)):
        start = pl.multiple_of((me ^ k) * own, own)
        down_grad[pl.ds(start, own), :] = piece[...].astype(F32)
    out_grad[...] = out[...].astype(F32)


def settle(me, pieces, out):
    own, group = out.shape
    return run(
        settle_kernel,
        [me],
        [*pieces, out],
        (
            jax.ShapeDtypeStruct((4 * own, group), F32),
            jax.ShapeDtypeStruct((own, group), F32),
        ),
        [],
        cost(10**6, 10**6),
    )


def columns_kernel(place_ref, u0, u1, u2, out):
    group = u0.shape[1]
    odd = place_ref[0] % 2
    out[:, group : 2 * group] = u1[...].astype(F32)

    @pl.when(odd == 0)
    def _():
        out[:, :group] = u0[...].astype(F32)
        out[:, 2 * group :] = u2[...].astype(F32)

    @pl.when(odd == 1)
    def _():
        out[:, :group] = u2[...].astype(F32)
        out[:, 2 * group :] = u0[...].astype(F32)


def columns(me, units):
    own, group = units[0].shape
    return run(
        columns_kernel,
        [me],
        [*units],
        (jax.ShapeDtypeStruct((own, 3 * group), F32),),
        [],
        cost(10**6, 10**6),
    )[0]


def body(
    frames_in,
    norm1_gain,
    norm1_bias,
    qkv_weight,
    query_bias,
    value_bias,
    out_weight,
    out_bias,
    norm2_gain,
    norm2_bias,
    up_weight,
    up_bias,
    down_weight,
    down_bias,
    cotangent,
):
    count = lax.axis_size("fsdp")
    q = count // GROUPS
    s = lax.axis_index("seq")
    f = lax.axis_index("fsdp")
    width = frames_in.shape[2]
    rows = frames_in.shape[0] * frames_in.shape[1]
    group = width // GROUPS
    own = qkv_weight.shape[0]
    hidden_all = up_weight.shape[1]
    hidden = hidden_all // GROUPS
    hid_own = down_weight.shape[0]
    ring = count == 8
    planes = count // 2 if ring else 1
    me = jnp.stack([s, f % 2, f // 2, f % GROUPS]).astype(jnp.int32)

    x = frames_in.reshape(rows, width)
    dy = cotangent.reshape(rows, width)

    vectors = jnp.concatenate(
        [
            norm1_gain,
            norm1_bias,
            query_bias,
            value_bias,
            out_bias,
            norm2_gain,
            norm2_bias,
            down_bias,
            up_bias,
        ]
    )
    lines = -(-vectors.shape[0] // width)
    padded = jnp.pad(vectors, (0, lines * width - vectors.shape[0])).reshape(lines, width)
    qkv_own = lax.dynamic_index_in_dim(
        qkv_weight.reshape(own, 3, GROUPS, group), s, 2, keepdims=False
    ).reshape(own, 3 * group)
    out_own = lax.dynamic_index_in_dim(
        out_weight.reshape(own, GROUPS, group), s, 1, keepdims=False
    )
    packed = jnp.concatenate([jnp.concatenate([qkv_own, out_own], 1), padded], 0)
    down_part = lax.dynamic_index_in_dim(
        down_weight.reshape(GROUPS, hid_own // GROUPS, width), s, 0, keepdims=False
    )
    up_own = lax.dynamic_slice_in_dim(up_weight, s * hidden, hidden, 1)
    x_pieces = [x] + [seq_swap(x, k) for k in (1, 2, 3)]
    down_own = to_groups(down_part, count)
    if ring:
        where, qkv_blocks = ring_gather(packed, count)
        vec = None
        pair = jnp.concatenate([up_own, down_own], 0)
        pair, *qkv_blocks = lax.optimization_barrier((pair, *qkv_blocks))
        up_blocks = ring_gather(pair, count)[1]
        down_blocks = []
    else:
        where = jnp.zeros((8,), jnp.int32)
        first = lax.all_gather(packed, "fsdp", axis=0, tiled=False)
        qkv_blocks = [first[:, :own, : 3 * group].reshape(width, 3 * group)]
        spread = first[:, own:].reshape(count, lines * width).astype(F32)
        gain1, bias1, qb, vb, bo, gain2, bias2, bd = (
            spread[:, i * own : (i + 1) * own].reshape(width) for i in range(8)
        )
        bu = spread[:, 8 * own : 8 * own + hid_own].reshape(hidden_all)
        bias = jnp.concatenate(
            [
                lax.dynamic_slice_in_dim(qb, s * group, group),
                jnp.zeros((group,), F32),
                lax.dynamic_slice_in_dim(vb, s * group, group),
                jnp.zeros((group,), F32),
            ]
        )
        bu = lax.dynamic_slice_in_dim(bu, s * hidden, hidden)
        vec = jnp.stack([gain1, bias1, bias, bo, gain2, bias2, bd, bu])
        second = lax.all_gather(
            jnp.concatenate([up_own, out_weight, down_own], 0), "fsdp", axis=0, tiled=False
        )
        up_blocks = [second[:, :own].reshape(width, hidden)]
        out_blocks = [second[:, own : 2 * own].reshape(width, width)]
        down_blocks = [second[:, 2 * own :].reshape(hidden, width)]

    act1, queries, keys, values, k_turned, v_turned, w_qkv, w_col, vec = project(
        where, me, x_pieces, qkv_blocks, vec, own, group
    )
    if ring:
        out_blocks = seq_pieces(w_col)
    o2, o3, lse_b = attend(1, queries, keys, v_turned)
    far2, far3 = seq_swap(o2, 2), seq_swap(o3, 3)
    queries_a = after(queries, o2)
    o0, o1, lse_a = attend(0, queries_a, keys, v_turned)
    o_pieces = [o0, seq_swap(o1, 1), far2, far3]
    dy_pieces = seq_pieces(after(dy, o2))
    h, act2, w_out = mix(where, me, vec, x, o_pieces, out_blocks, own, group)
    a_pieces = seq_pieces(act2)
    g_a, du_a, part0, part1, usum_a, w_up, w_down = feed(
        where, vec, a_pieces[:2], dy_pieces[:2], up_blocks, down_blocks, own
    )
    near0 = seq_swap(part1, 1)
    g_b, du_b, part2, part3, usum_b, _, _ = feed(
        where, vec, a_pieces[2:], dy_pieces[2:], [w_up], [w_down], own
    )
    near2 = seq_swap(part3, 1)
    far_sum = (part2 + near2.astype(F32)).astype(BF)
    far = seq_swap(far_sum, 2)

    du_late = after(du_b, far_sum)
    feed_parts = feed_grads(
        me, a_pieces, dy_pieces, (g_a, g_b), (du_a, du_late), own, planes
    )
    if ring:
        up_keep, up_give, down_keep, down_give = feed_parts
        up_got = side_swap(up_give, count)
        down_got = side_swap(down_give, count)
    far = after(far, feed_parts[0])
    dh, db, d0, d1, d2, d3, sums2 = turn(me, vec, h, dy, part0, near0, far, w_out, group)
    near1 = seq_swap(d1, 1)
    far2, far3 = seq_swap(d2, 2), seq_swap(d3, 3)
    y_parts = feed_out((g_a, after(g_b, d3)), w_down)
    lse_a = after(lse_a, y_parts[0])
    back_a = back_first(queries, keys, values, k_turned, lse_a, d0, near1)
    y_near = seq_swap(y_parts[2], 1)
    db_pieces = seq_pieces(after(db, y_parts[0]))
    y_sum = (y_parts[1] + y_near[rows:].astype(F32)).astype(BF)
    y_far = seq_swap(y_sum, 2)
    lse_b = after(lse_b, back_a[0], y_sum)
    if ring:
        up_got, down_got, lse_b = lax.optimization_barrier((up_got, down_got, lse_b))
        (up_own_sum, *up_sends), (down_own_sum, *down_sends) = plane_parts(
            me, [(up_keep, up_got), (down_keep, down_got)]
        )
        up_arrived = plane_swaps(up_sends, count)
        down_arrived = plane_swaps(down_sends, count)
        lse_b = after(lse_b, up_own_sum)
    dqkv, *qkv_parts = back_second(
        me,
        queries,
        keys,
        values,
        k_turned,
        lse_b,
        (far2, far3),
        back_a,
        act1,
        (o0, o1, o2, o3),
        db_pieces,
        own,
        planes,
    )
    if ring:
        qkv_got = side_swap(qkv_parts[1], count)
    part0, part2, sent1, sent3, sums1 = project_back(
        me, after(dqkv, qkv_parts[0]), w_qkv, x_pieces
    )
    near_a, near_b = seq_swap(sent1, 1), seq_swap(sent3, 1)
    far_sum = (part2 + near_b.astype(F32)).astype(BF)
    far1 = seq_swap(far_sum, 2)
    if ring:
        vec_keep, vec_give = pack(me, sums1, sums2, usum_a, usum_b, own)
        vec_got = side_swap(vec_give, count)
        qkv_got = after(qkv_got, vec_keep, far_sum)
        (qkv_own_sum, *qkv_sends), = plane_parts(me, [(qkv_parts[0], qkv_got)])
        qkv_arrived = plane_swaps(qkv_sends, count)
        vectors = after(vec_keep + vec_got, qkv_own_sum)
        for step in (2, 4):
            vectors = vectors + lax.ppermute(
                vectors, "fsdp", [(i, i ^ step) for i in range(count)]
            )
        up_own_sum = after(up_own_sum, qkv_own_sum)
        grad_up, *down_columns = feed_sums(
            me, up_own_sum, up_arrived, down_own_sum, down_arrived
        )
        down_columns = [to_owners(piece, count, k) for k, piece in enumerate(down_columns)]
        far1 = after(far1, grad_up)
    y_far = after(y_far, far1)
    layer_out = h + (y_parts[0] + y_near[:rows].astype(F32) + y_far.astype(F32)) + vec[6]
    layer_out = layer_out.astype(BF).reshape(frames_in.shape)
    input_grad = finish(vec, x, dh, part0, near_a, far1).reshape(frames_in.shape)
    if ring:
        *units, out_block = unpack(me, after(qkv_own_sum, input_grad), qkv_arrived)
        units = [units[0], seq_swap(units[1], 1), seq_swap(units[2], 2)]
        out_block = to_owners(out_block, count, 0)
        vectors = lax.dynamic_index_in_dim(vectors, f // 2, 0, keepdims=False)
        vectors = vectors + seq_swap(vectors, 1)
        vectors = vectors + seq_swap(vectors, 2)
        grad_qkv = columns(me, units)
        grad_down, grad_out = settle(me, down_columns, out_block)
        g_gain1, g_bias1, g_query, g_value, g_outb, g_gain2, g_bias2, g_downb = (
            vectors[i * own : (i + 1) * own] for i in range(8)
        )
        g_upb = vectors[8 * own :]
    else:
        units = fsdp_reduce(qkv_parts[0].reshape(count, own, 3 * group)).astype(BF)
        units = units.reshape(own, 3, group)
        order = jnp.array([[0, 1, 2], [1, 0, 2], [1, 2, 0], [2, 1, 0]], jnp.int32)[s]
        got = [lax.dynamic_index_in_dim(units, order[k], 1, keepdims=False) for k in range(3)]
        got = [got[0], seq_swap(got[1], 1), seq_swap(got[2], 2)]
        odd = s % 2 == 1
        grad_qkv = jnp.concatenate(
            [jnp.where(odd, got[2], got[0]), got[1], jnp.where(odd, got[0], got[2])], 1
        ).astype(F32)
        grad_up = fsdp_reduce(feed_parts[0].reshape(count, own, hidden))
        grad_down = fsdp_reduce(feed_parts[1].reshape(count, own, width)).astype(BF)
        out_parts = out_grads(me, [o0, o1, o2, o3], db_pieces, own)
        grad_out = to_owners(fsdp_reduce(out_parts[0]).astype(BF), count, 0).astype(F32)
        split = grad_down.reshape(own, GROUPS, group)
        pieces = jnp.stack(
            [
                to_owners(
                    lax.dynamic_index_in_dim(split, (f % GROUPS) ^ k, 1, keepdims=False), count, k
                )
                for k in range(GROUPS)
            ]
        )
        grad_down = jnp.concatenate(
            [lax.dynamic_index_in_dim(pieces, t ^ s, 0, keepdims=False) for t in range(GROUPS)], 0
        ).astype(F32)

        def placed(values, size):
            return lax.dynamic_update_slice_in_dim(
                jnp.zeros((size,), F32), values, s * values.shape[0], 0
            ).reshape(count, size // count)

        sums = [
            sums1[0].reshape(count, own),
            sums1[1].reshape(count, own),
            placed(sums1[2, :group], width),
            placed(sums1[2, 2 * group : 3 * group], width),
            sums2[0].reshape(count, own),
            sums2[1].reshape(count, own),
            sums2[2].reshape(count, own),
            sums2[3].reshape(count, own),
            placed(usum_a[0] + usum_b[0], hidden_all),
        ]
        total = lax.psum(fsdp_reduce(jnp.concatenate(sums, 1)), "seq")
        g_gain1, g_bias1, g_query, g_value, g_outb, g_gain2, g_bias2, g_downb = (
            total[i * own : (i + 1) * own] for i in range(8)
        )
        g_upb = total[8 * own :]

    return (
        layer_out,
        input_grad,
        g_gain1,
        g_bias1,
        grad_qkv,
        g_query,
        g_value,
        grad_out,
        g_outb,
        g_gain2,
        g_bias2,
        grad_up,
        g_upb,
        grad_down,
        g_downb,
    )


def solution(mesh):
    tokens = P("fsdp", "seq", None)
    vector = P("fsdp")
    matrix = P("fsdp", None)
    summed = P("fsdp", "seq")
    return jax.shard_map(
        body,
        mesh=mesh,
        in_specs=(
            tokens,
            vector,
            vector,
            matrix,
            vector,
            vector,
            matrix,
            vector,
            vector,
            vector,
            matrix,
            vector,
            matrix,
            vector,
            tokens,
        ),
        out_specs=(
            tokens,
            tokens,
            vector,
            vector,
            summed,
            vector,
            vector,
            summed,
            vector,
            vector,
            vector,
            summed,
            vector,
            summed,
            vector,
        ),
        check_vma=False,
    )
```

```python
import functools

import jax
import jax.numpy as jnp
from jax import lax
from jax.experimental import pallas as pl
from jax.experimental.pallas import tpu as pltpu
from jax.sharding import PartitionSpec as P

HD = 64
GROUPS = 4
epsilon = 1e-05
BF = jnp.bfloat16
F32 = jnp.float32


def dot(a, b):
    return jnp.dot(a, b, preferred_element_type=F32)


def dot_tn(a, b):
    return lax.dot_general(a, b, (((0,), (0,)), ((), ())), preferred_element_type=F32)


def dot_nt(a, b):
    return lax.dot_general(a, b, (((1,), (1,)), ((), ())), preferred_element_type=F32)


def seq_swap(value, step):
    return lax.ppermute(value, "seq", [(i, i ^ step) for i in range(GROUPS)])


def seq_pieces(value):
    near = seq_swap(value, 1)
    far = seq_swap(value, 2)
    return [value, near, far, seq_swap(far, 1)]


def fsdp_reduce(blocks):
    return lax.psum_scatter(blocks, "fsdp", scatter_dimension=0, tiled=False)


def side_swap(value, count):
    return lax.ppermute(value, "fsdp", [(i, i ^ 1) for i in range(count)])


def plane_swaps(parts, count):
    return [
        lax.ppermute(part, "fsdp", [(i, i ^ (2 * step)) for i in range(count)])
        for step, part in enumerate(parts, 1)
    ]


def add_all(own, arrived):
    for part in arrived:
        own = own + part.astype(F32)
    return own


def ring_order(count):
    return list(range(0, count, 2)) + list(range(count - 1, 0, -2))


def ring_gather(value, count):
    order = ring_order(count)
    ahead = [(order[i], order[(i + 1) % count]) for i in range(count)]
    back = [(b, a) for a, b in ahead]
    half = value.shape[0] // 32 * 16
    blocks, shifts = [value], [0]
    left = right = value
    for step in range(1, count // 2):
        left = lax.ppermute(left, "fsdp", ahead)
        right = lax.ppermute(right, "fsdp", back)
        blocks += [left, right]
        shifts += [-step, step]
    last = [lax.ppermute(left[:half], "fsdp", ahead), lax.ppermute(right[half:], "fsdp", back)]
    blocks.append(jnp.concatenate(last, 0))
    shifts.append(count // 2)
    spot = jnp.array([order.index(i) for i in range(count)], jnp.int32)[lax.axis_index("fsdp")]
    sources = jnp.array(order, jnp.int32)[(spot + jnp.array(shifts, jnp.int32)) % count]
    return sources, blocks


def after(value, *others):
    return lax.optimization_barrier((value,) + others)[0]


def to_groups(value, count):
    q = count // GROUPS
    pairs = []
    for s in range(GROUPS):
        for j in range(q):
            for t in range(GROUPS):
                pairs.append(((q * s + j) * GROUPS + t, (GROUPS * j + t) * GROUPS + s))
    return lax.ppermute(value, ("fsdp", "seq"), pairs)


def to_owners(value, count, step):
    q = count // GROUPS
    pairs = []
    for s in range(GROUPS):
        for j in range(q):
            for t in range(GROUPS):
                pairs.append(
                    ((GROUPS * j + t) * GROUPS + s, (q * s + j) * GROUPS + (t ^ step))
                )
    return lax.ppermute(value, ("fsdp", "seq"), pairs)


def normalise(values):
    center = values - jnp.mean(values, -1, keepdims=True)
    rstd = lax.rsqrt(jnp.mean(center * center, -1, keepdims=True) + epsilon)
    return center * rstd, rstd


def norm_back(grad, gain, xhat, rstd):
    e = grad * gain
    return rstd * (
        e - jnp.mean(e, -1, keepdims=True) - xhat * jnp.mean(e * xhat, -1, keepdims=True)
    )


def params(megabytes=26):
    return pltpu.CompilerParams(vmem_limit_bytes=megabytes * 2**20)


SMEM = pl.BlockSpec(memory_space=pltpu.SMEM)
VMEM = pl.BlockSpec(memory_space=pltpu.VMEM)
ANY = pl.BlockSpec(memory_space=pl.ANY)


def run(kernel, scalars, arrays, out_shape, scratch, megabytes, micros, direct=False):
    n_scalars, n_arrays, n_outs = len(scalars), len(arrays), len(out_shape)

    estimate = pl.CostEstimate(
        flops=int(micros * 10**9), bytes_accessed=2**20, transcendentals=0
    )
    if direct:
        return pl.pallas_call(
            kernel,
            out_shape=tuple(out_shape),
            in_specs=[SMEM] * n_scalars + [VMEM] * n_arrays,
            out_specs=(VMEM,) * n_outs,
            scratch_shapes=list(scratch),
            compiler_params=params(megabytes),
            cost_estimate=estimate,
        )(*scalars, *arrays)

    def wrapped(*refs):
        rest = refs[n_scalars + n_arrays :]
        outs, own = rest[:n_outs], rest[n_outs : n_outs + len(scratch)]
        held, sems = rest[n_outs + len(scratch) : -1], rest[-1]
        copies = [
            pltpu.make_async_copy(refs[n_scalars + i], held[i], sems.at[i])
            for i in range(n_arrays)
        ]
        for copy in copies:
            copy.start()
        for copy in copies:
            copy.wait()
        kernel(*refs[:n_scalars], *held, *outs, *own)

    return pl.pallas_call(
        wrapped,
        out_shape=tuple(out_shape),
        in_specs=[SMEM] * n_scalars + [ANY] * n_arrays,
        out_specs=(VMEM,) * n_outs,
        scratch_shapes=list(scratch)
        + [pltpu.VMEM(a.shape, a.dtype) for a in arrays]
        + [pltpu.SemaphoreType.DMA((n_arrays,))],
        compiler_params=params(megabytes),
        cost_estimate=estimate,
    )(*scalars, *arrays)


def lane_ids(width):
    return lax.broadcasted_iota(jnp.int32, (1, width), 1)


def collect_vectors(where, me, blocks, own, group, vec, table):
    count = len(blocks)
    width = count * own
    table[...] = jnp.zeros_like(table)
    for i, block in enumerate(blocks):
        pair = block[own : own + 2, :].astype(F32)
        table[0, pl.ds(where[i], 1), :] = pair[0:1]
        table[1, pl.ds(where[i], 1), :] = pair[1:2]
    lanes = lax.broadcasted_iota(jnp.int32, (count, width), 1)
    rows = lax.broadcasted_iota(jnp.int32, (count, width), 0)
    mine = (lanes >= rows * own) & (lanes < (rows + 1) * own)
    base = table[0]
    shifted_base = [base] + [pltpu.roll(base, k * own, 1) for k in range(1, count)]

    def whole(index, shifted=None):
        shifted = shifted or shifted_base
        picked = jnp.zeros((count, width), F32)
        for k in range(count):
            here = mine & (rows == (k + index) % count)
            picked = jnp.where(here, shifted[k], picked)
        return jnp.sum(picked, 0, keepdims=True)

    gain1, bias1, qb, vb, bo, gain2, bias2, bd = (whole(i) for i in range(8))
    lane = lane_ids(width)
    qb = pltpu.roll(qb, lax.rem(width - me * group, width), 1)
    vb = pltpu.roll(vb, lax.rem(width + 2 * group - me * group, width), 1)
    bias = jnp.where(lane < group, qb, 0.0)
    bias = jnp.where((lane >= 2 * group) & (lane < 3 * group), vb, bias)
    units = pltpu.roll(table[1], lax.rem(width - me * own, width), 1)
    shifted = [units] + [pltpu.roll(units, k * own, 1) for k in range(1, count)]
    bu = whole(0, shifted)
    for i, row in enumerate((gain1, bias1, bias, bo, gain2, bias2, bd, bu)):
        vec[i : i + 1, :] = row


def units_kernel(own, place_ref, up, down, pair):
    me = place_ref[0]
    count = up.shape[1] // (4 * own)
    for s in range(4):

        @pl.when(me == s)
        def _(s=s):
            for f in range(count):
                start = (4 * f + s) * own
                pair[:own, f * own : (f + 1) * own] = up[:, start : start + own]
            pair[own:, :] = down[s * own : (s + 1) * own, :]


def own_units(me, up, down):
    own, width = up.shape[0], down.shape[1]
    return run(
        functools.partial(units_kernel, own),
        [me],
        [up, down],
        (jax.ShapeDtypeStruct((2 * own, width), BF),),
        [],
        8,
        3.0,
    )[0]


def project_kernel(ring, own, group, rows, *refs):
    where, place_ref = refs[0], refs[1]
    x_refs = refs[2:6]
    n_blocks = 8 if ring else 1
    blocks = refs[6 : 6 + n_blocks]
    rest = refs[6 + n_blocks :]
    if not ring:
        vec_in, rest = rest[0], rest[1:]
    act, queries, keys, values, k_turned, v_turned, w, w_col, vec, kept, table = rest
    me = place_ref[0]
    heads = group // HD
    if ring:
        collect_vectors(where, me, blocks, own, group, vec, table)
    else:
        vec[...] = vec_in[...]
    if ring:
        for i, block in enumerate(blocks):
            start = pl.multiple_of(where[i] * own, own)
            w[pl.ds(start, own), :] = block[:own, : 3 * group]
            w_col[pl.ds(start, own), :] = block[:own, 3 * group :]
    else:
        w[...] = blocks[0][...]
        w_col[...] = jnp.zeros_like(w_col)
    gain, shift, bias = vec[0:1, :], vec[1:2, :], vec[2:3, : 3 * group]
    for k in range(4):
        here = slice(k * rows, (k + 1) * rows)
        values_in = x_refs[k][...]
        kept[here, :] = values_in
        xhat, _ = normalise(values_in.astype(F32))
        block = (xhat * gain + shift).astype(BF)
        act[here, :] = block
        qkv = (dot(block, w[...]) + bias).astype(BF)
        queries[here, :] = qkv[:, :group] * jnp.asarray(HD ** (-0.5), BF)
        for head in range(heads):
            keys[head, here, :] = qkv[:, group + head * HD : group + (head + 1) * HD]
            values[head, here, :] = qkv[:, 2 * group + head * HD : 2 * group + (head + 1) * HD]
        k_turned[:, here] = qkv[:, group : 2 * group].T
        v_turned[:, here] = qkv[:, 2 * group : 3 * group].T


def project(where, me, pieces, blocks, vec, own, group):
    rows, width = pieces[0].shape
    frames = 4 * rows
    heads = group // HD
    ring = len(blocks) > 1
    out_shape = (
        jax.ShapeDtypeStruct((frames, width), BF),
        jax.ShapeDtypeStruct((frames, group), BF),
        jax.ShapeDtypeStruct((heads, frames, HD), BF),
        jax.ShapeDtypeStruct((heads, frames, HD), BF),
        jax.ShapeDtypeStruct((group, frames), BF),
        jax.ShapeDtypeStruct((group, frames), BF),
        jax.ShapeDtypeStruct((width, 3 * group), BF),
        jax.ShapeDtypeStruct((width, group), BF),
        jax.ShapeDtypeStruct((8, width), F32),
        jax.ShapeDtypeStruct((frames, width), BF),
    )
    args = [where, me, *pieces, *blocks] + ([] if ring else [vec])
    return run(
        functools.partial(project_kernel, ring, own, group, rows),
        args[:2],
        args[2:],
        out_shape,
        [pltpu.VMEM((2, 8, width), F32)],
        16,
        9.0,
        direct=True,
    )


def attend_kernel(group, rows, part, queries, keys, v_turned, first, second, lse):
    heads = group // HD
    lse[...] = jnp.zeros_like(lse)
    for t, out in enumerate((first, second)):
        turned = []
        for head in range(heads):
            start = (2 * part + t) * rows
            query = queries[start : start + rows, head * HD : (head + 1) * HD]
            scores = dot_nt(keys[head], query)
            top = jnp.max(scores, 0, keepdims=True)
            e = jnp.exp(scores - top)
            total = jnp.sum(e, 0, keepdims=True)
            lse[head : head + 1, t * rows : (t + 1) * rows] = top + jnp.log(total)
            p = (e * (1.0 / total)).astype(BF)
            turned.append(dot(v_turned[head * HD : (head + 1) * HD, :], p))
        out[...] = jnp.concatenate(turned, 0).T.astype(BF)


def attend(part, queries, keys, v_turned):
    frames, group = queries.shape
    rows = frames // 4
    return run(
        functools.partial(attend_kernel, group, rows, part),
        [],
        [queries, keys, v_turned],
        (
            jax.ShapeDtypeStruct((rows, group), BF),
            jax.ShapeDtypeStruct((rows, group), BF),
            jax.ShapeDtypeStruct((8, 2 * rows), F32),
        ),
        [],
        10,
        7.5,
    )


def mix_kernel(own, group, rows, *refs):
    where, place_ref, vec, x = refs[:4]
    o_refs = refs[4:8]
    blocks, (h, act, w) = refs[8:-3], refs[-3:]
    me = place_ref[0]
    if len(blocks) == 1:
        w[...] = blocks[0][...]
    else:
        for k, block in enumerate(blocks):
            for c in range(4):

                @pl.when((me ^ k) == c)
                def _(block=block, c=c):
                    w[:, c * group : (c + 1) * group] = block[...]

    total = x[...].astype(F32) + vec[3:4, :]
    for k in range(4):
        start = pl.multiple_of((me ^ k) * group, group)
        total = total + dot(o_refs[k][:rows, :], w[pl.ds(start, group), :])
    h[...] = total
    xhat, _ = normalise(total)
    act[...] = (xhat * vec[4:5, :] + vec[5:6, :]).astype(BF)


def mix(where, me, vec, x, pieces, blocks, own, group):
    rows, width = x.shape
    args = [where, me, vec, x, *pieces, *blocks]
    return run(
        functools.partial(mix_kernel, own, group, rows),
        args[:2],
        args[2:],
        (
            jax.ShapeDtypeStruct((rows, width), F32),
            jax.ShapeDtypeStruct((rows, width), BF),
            jax.ShapeDtypeStruct((width, width), BF),
        ),
        [],
        10,
        6.0,
    )


def feed_kernel(n_up, n_down, own, rows, *refs):
    where, vec, a0, a1, dy0, dy1 = refs[:6]
    ups = refs[6 : 6 + n_up]
    downs = refs[6 + n_up : 6 + n_up + n_down]
    g, du, first, second, total, w_up, w_down = refs[6 + n_up + n_down :]
    if n_down:
        w_up[...] = ups[0][...]
        w_down[...] = downs[0][...]
    elif len(ups) == 1:
        for i in range(w_up.shape[0] // own):
            here = slice(i * own, (i + 1) * own)
            w_up[here, :] = ups[0][2 * i * own : (2 * i + 1) * own, :]
            w_down[here, :] = ups[0][(2 * i + 1) * own : (2 * i + 2) * own, :]
    else:
        for i, block in enumerate(ups):
            start = pl.multiple_of(where[i] * own, own)
            skip = block.shape[0] - 2 * own
            w_up[pl.ds(start, own), :] = block[skip : skip + own, :]
            w_down[pl.ds(start, own), :] = block[skip + own :, :]
    bias = vec[7:8, :]
    total[...] = jnp.zeros_like(total)
    chunk = rows // 2
    for part, (a, dy, out) in enumerate(((a0, dy0, first), (a1, dy1, second))):
        for c in range(2):
            here = slice(c * chunk, (c + 1) * chunk)
            there = slice(part * rows + c * chunk, part * rows + (c + 1) * chunk)
            u = dot(a[here, :], w_up[...]) + bias
            cdf = 0.5 * (1.0 + lax.erf(u * (0.5**0.5)))
            pdf = jnp.exp(-0.5 * u * u) * ((2.0 * jnp.pi) ** (-0.5))
            g[there, :] = (u * cdf).astype(BF)
            grad = (dot_nt(dy[here, :], w_down[...]) * (cdf + u * pdf)).astype(BF)
            du[there, :] = grad
            total[0:1, :] += jnp.sum(grad.astype(F32), 0, keepdims=True)
            out[here, :] = dot_nt(grad, w_up[...]).astype(out.dtype)


def feed(where, vec, acts, dys, ups, downs, own):
    rows, width = acts[0].shape
    hidden = ups[0].shape[1]
    assert width == hidden
    args = [where, vec, *acts, *dys, *ups, *downs]
    return run(
        functools.partial(feed_kernel, len(ups), len(downs), own, rows),
        args[:1],
        args[1:],
        (
            jax.ShapeDtypeStruct((2 * rows, hidden), BF),
            jax.ShapeDtypeStruct((2 * rows, hidden), BF),
            jax.ShapeDtypeStruct((rows, width), F32),
            jax.ShapeDtypeStruct((rows, width), BF),
            jax.ShapeDtypeStruct((8, hidden), F32),
            jax.ShapeDtypeStruct((width, hidden), BF),
            jax.ShapeDtypeStruct((hidden, width), BF),
        ),
        [],
        18,
        8.2,
    )


def feed_out_kernel(rows, g_a, g_b, w, first, third, sent):
    for k in (1, 3, 0, 2):
        here = slice((k % 2) * rows, (k % 2 + 1) * rows)
        part = dot((g_a if k < 2 else g_b)[here, :], w[...])
        if k == 0:
            first[...] = part
        elif k == 2:
            third[...] = part
        else:
            sent[(k // 2) * rows : (k // 2 + 1) * rows, :] = part.astype(BF)


def feed_out(gs, w):
    rows = gs[0].shape[0] // 2
    width = w.shape[1]
    return run(
        functools.partial(feed_out_kernel, rows),
        [],
        [*gs, w],
        (
            jax.ShapeDtypeStruct((rows, width), F32),
            jax.ShapeDtypeStruct((rows, width), F32),
            jax.ShapeDtypeStruct((2 * rows, width), BF),
        ),
        [],
        10,
        3.0,
    )


def turn_kernel(*refs):
    vec, h, dy, part, near, far = refs[1:7]
    dh, db, sums = refs[7:]
    da = part[...] + near[...].astype(F32) + far[...].astype(F32)
    xhat, rstd = normalise(h[...])
    cot = dy[...].astype(F32)
    grad = cot + norm_back(da, vec[4:5, :], xhat, rstd)
    dh[...] = grad
    low = grad.astype(BF)
    db[...] = low
    sums[...] = jnp.zeros_like(sums)
    sums[0:1, :] = jnp.sum(low.astype(F32), 0, keepdims=True)
    sums[1:2, :] = jnp.sum(da * xhat, 0, keepdims=True)
    sums[2:3, :] = jnp.sum(da, 0, keepdims=True)
    sums[3:4, :] = jnp.sum(cot, 0, keepdims=True)


def turn(me, vec, h, dy, part, near, far):
    rows, width = h.shape
    return run(
        turn_kernel,
        [me],
        [vec, h, dy, part, near, far],
        (
            jax.ShapeDtypeStruct((rows, width), F32),
            jax.ShapeDtypeStruct((rows, width), BF),
            jax.ShapeDtypeStruct((8, width), F32),
        ),
        [],
        10,
        3.0,
    )


def back_tiles(me, group, rows, part, qkv, lse, db_refs, w, dk, dv, dq, skip):
    queries, keys, values, k_turned = qkv
    heads = group // HD
    for t in range(2):
        start = (2 * part + t) * rows
        turned = []
        w_own = w[pl.ds(pl.multiple_of(me * group, group), group), :]
        d_all = dot_nt(db_refs[t][...], w_own).astype(BF)
        for head in range(heads):
            here = slice(head * HD, (head + 1) * HD)
            query = queries[start : start + rows, here]
            d_out = d_all[:, here]
            scores = dot_nt(keys[head], query)
            p = jnp.exp(scores - lse[head : head + 1, t * rows : (t + 1) * rows])
            dv[head] += dot(p.astype(BF), d_out)
            dp = dot_nt(values[head], d_out)
            inner = jnp.sum(p * dp, 0, keepdims=True)
            ds = (p * (dp - inner)).astype(BF)
            dk[head] += dot(ds, query)
            turned.append(dot(k_turned[here, :], ds))
        dq[skip + t * rows : skip + (t + 1) * rows, :group] = (
            jnp.concatenate(turned, 0).T * HD ** (-0.5)
        ).astype(BF)


def back_first_kernel(group, rows, place_ref, *refs):
    qkv, (lse, db0, db1, w, dq, dk, dv) = refs[:4], refs[4:]
    dk[...] = jnp.zeros_like(dk)
    dv[...] = jnp.zeros_like(dv)
    back_tiles(place_ref[0], group, rows, 0, qkv, lse, (db0, db1), w, dk, dv, dq, 0)


def back_first(me, queries, keys, values, k_turned, lse, dbs, w):
    frames, group = queries.shape
    heads = group // HD
    total = jax.ShapeDtypeStruct((heads, frames, HD), F32)
    return run(
        functools.partial(back_first_kernel, group, frames // 4),
        [me],
        [queries, keys, values, k_turned, lse, *dbs, w],
        (jax.ShapeDtypeStruct((frames // 2, group), BF), total, total),
        [],
        18,
        12.0,
    )


def back_second_kernel(group, rows, place_ref, *refs):
    qkv, (lse, w, dq_first, dk_first, dv_first, db2, db3) = refs[:4], refs[4:11]
    dqkv, dk, dv = refs[11:]
    heads = group // HD
    dk[...] = dk_first[...]
    dv[...] = dv_first[...]
    dqkv[: 2 * rows, :group] = dq_first[...]
    dbs = (db2, db3)
    back_tiles(place_ref[0], group, rows, 1, qkv, lse, dbs, w, dk, dv, dqkv, 2 * rows)
    dqkv[:, group : 2 * group] = jnp.concatenate([dk[i] for i in range(heads)], 1).astype(BF)
    dqkv[:, 2 * group :] = jnp.concatenate([dv[i] for i in range(heads)], 1).astype(BF)


def back_second(me, queries, keys, values, k_turned, lse, w, first, dbs):
    frames, group = queries.shape
    heads = group // HD
    return run(
        functools.partial(back_second_kernel, group, frames // 4),
        [me],
        [queries, keys, values, k_turned, lse, w, *first, *dbs],
        (jax.ShapeDtypeStruct((frames, 3 * group), BF),),
        [pltpu.VMEM((heads, frames, HD), F32), pltpu.VMEM((heads, frames, HD), F32)],
        20,
        12.0,
    )[0]


def feed_grads_kernel(own, rows, *refs):
    acts, dys = refs[:4], refs[4:8]
    g_a, g_b, du_a, du_b = refs[8:12]
    out = refs[12]
    up, down = 0.0, 0.0
    for k in range(4):
        here = slice((k % 2) * rows, (k % 2 + 1) * rows)
        up = up + dot_tn(acts[k][...], (du_a if k < 2 else du_b)[here, :])
    for f in range(out.shape[0]):
        out[f, :own, :] = up[f * own : (f + 1) * own, :].astype(BF)
    for k in range(4):
        here = slice((k % 2) * rows, (k % 2 + 1) * rows)
        down = down + dot_tn((g_a if k < 2 else g_b)[here, :], dys[k][...])
    for f in range(out.shape[0]):
        out[f, own:, :] = down[f * own : (f + 1) * own, :].astype(BF)


def feed_grads(acts, dys, gs, dus, own):
    rows, width = acts[0].shape
    return run(
        functools.partial(feed_grads_kernel, own, rows),
        [],
        [*acts, *dys, *gs, *dus],
        (jax.ShapeDtypeStruct((width // own, 2 * own, width), BF),),
        [],
        20,
        9.0,
    )[0]


def out_grads_kernel(own, group, *refs):
    o_refs, db_refs, blocks = refs[1:5], refs[5:9], refs[9]
    total = 0.0
    for k in range(4):
        total = total + dot_tn(o_refs[k][...], db_refs[k][...])
    for j in range(group // own):
        for t in range(4):
            blocks[j * 4 + t] = total[j * own : (j + 1) * own, t * group : (t + 1) * group]


def out_grads(me, os, dbs, own):
    group = os[0].shape[1]
    return run(
        functools.partial(out_grads_kernel, own, group),
        [me],
        [*os, *dbs],
        (jax.ShapeDtypeStruct((group // own * 4, own, group), F32),),
        [],
        12,
        3.0,
    )


def plane_kernel(own, place_ref, keep, got, *outs):
    plane = place_ref[2]
    for step, out in enumerate(outs):
        z = plane ^ step
        total = keep[z, :own, :] + got[z, :own, :].astype(F32)
        lines = keep[z, own:, :] + got[z, own : own + 8, :].astype(F32)
        lines = lines + got[z, own + 8 :, :].astype(F32)
        if step == 0:
            out[:own, :] = total
            out[own:, :] = lines
        else:
            out[:own, :] = total.astype(BF)
            high, low = split_low(lines)
            out[own : own + 8, :] = high
            out[own + 8 :, :] = low


def plane_parts(me, keep, got):
    planes, height, width = keep.shape
    out_shape = [jax.ShapeDtypeStruct((height, width), F32)]
    out_shape += [jax.ShapeDtypeStruct((height + 8, width), BF)] * (planes - 1)
    return run(
        functools.partial(plane_kernel, height - 8),
        [me],
        [keep, got],
        tuple(out_shape),
        [],
        12,
        2.2,
    )


def split_low(value):
    high = value.astype(BF)
    return high, (value - high.astype(F32)).astype(BF)


def close_kernel(own, group, rows, split, place_ref, dqkv, act, w, x, *refs):
    o_refs, db_refs = refs[:4], refs[4:8]
    sums2, usum_a, usum_b = refs[8:11]
    if split:
        keep, give, first, third, sent, table, lines, grads = refs[11:]
    else:
        grads, first, third, sent, sums = refs[11:]
    width = w.shape[0]
    gain_sum, shift_sum = 0.0, 0.0
    for k in (1, 3, 0, 2):
        part = dot_nt(dqkv[k * rows : (k + 1) * rows, :], w[...])
        xhat, _ = normalise(x[k * rows : (k + 1) * rows, :].astype(F32))
        gain_sum = gain_sum + jnp.sum(part * xhat, 0, keepdims=True)
        shift_sum = shift_sum + jnp.sum(part, 0, keepdims=True)
        if k == 0:
            first[...] = part
        elif k == 2:
            third[...] = part
        else:
            sent[(k // 2) * rows : (k // 2 + 1) * rows, :] = part.astype(BF)
    dsum = jnp.sum(dqkv[...].astype(F32), 0, keepdims=True)
    if not split:
        sums[...] = jnp.zeros_like(sums)
        sums[0:1, :] = gain_sum
        sums[1:2, :] = shift_sum
        sums[2:3, : 3 * group] = dsum
        grads[...] = dot_tn(act[...], dqkv[...])
        return
    me, side = place_ref[0], place_ref[1]
    out = 0.0
    for k in range(4):
        out = out + dot_tn(o_refs[k][...], db_refs[k][...])
    for j in range(2):
        for t in range(4):
            start = (j * 4 + t) * own
            grads[start : start + own, 3 * group :] = out[
                j * own : (j + 1) * own, t * group : (t + 1) * group
            ]
    grads[:, : 3 * group] = dot_tn(act[...], dqkv[...])
    count = width // own
    lane = lane_ids(width)
    table[0:1, :] = gain_sum
    table[1:2, :] = shift_sum
    table[3:4, :] = jnp.zeros((1, width), F32)
    table[3:4, : 3 * group] = dsum
    spread = table[3:4, :]
    query = jnp.where(lane < group, spread, 0.0)
    value = jnp.where(lane < group, pltpu.roll(spread, 2 * group, 1), 0.0)
    table[2:3, :] = pltpu.roll(query, me * group, 1)
    table[3:4, :] = pltpu.roll(value, me * group, 1)
    table[4:8, :] = sums2[0:4, :]
    base = table[...]
    shifted = [base] + [pltpu.roll(base, k * own, 1) for k in range(1, count)]
    lanes = lax.broadcasted_iota(jnp.int32, (count, width), 1)
    ids = lax.broadcasted_iota(jnp.int32, (count, width), 0)
    mine = (lanes >= ids * own) & (lanes < (ids + 1) * own)
    units = pltpu.roll(usum_a[0:1, :] + usum_b[0:1, :], me * own, 1)
    inside = (lane >= me * own) & (lane < (me + 1) * own)
    for f in range(count):
        picked = jnp.zeros((count, width), F32)
        for k in range(count):
            picked = jnp.where(mine & (ids == (f + k) % count), shifted[k], picked)
        lines[f, 0:1, :] = jnp.sum(picked, 0, keepdims=True)
        turned = units if f == 0 else pltpu.roll(units, width - f * own, 1)
        lines[f, 1:2, :] = jnp.where(inside, turned, 0.0)
    for z in range(count // 2):
        mine_f, other = 2 * z + side, 2 * z + 1 - side
        keep[z, :own, :] = grads[pl.ds(pl.multiple_of(mine_f * own, own), own), :]
        keep[z, own:, :] = lines[mine_f]
        rest = grads[pl.ds(pl.multiple_of(other * own, own), own), :]
        give[z, :own, :] = rest.astype(BF)
        high, low = split_low(lines[other])
        give[z, own : own + 8, :] = high
        give[z, own + 8 :, :] = low


def close(me, dqkv, act, w, x, os, dbs, sums2, usum_a, usum_b, own, planes):
    rows, width = x.shape[0] // 4, x.shape[1]
    group = width // 4
    split = planes > 1
    out_shape = (
        jax.ShapeDtypeStruct((rows, width), F32),
        jax.ShapeDtypeStruct((rows, width), F32),
        jax.ShapeDtypeStruct((2 * rows, width), BF),
    )
    if split:
        out_shape = (
            jax.ShapeDtypeStruct((planes, own + 8, width), F32),
            jax.ShapeDtypeStruct((planes, own + 16, width), BF),
        ) + out_shape
        scratch = [
            pltpu.VMEM((8, width), F32),
            pltpu.VMEM((2 * planes, 8, width), F32),
            pltpu.VMEM((width, width), F32),
        ]
    else:
        out_shape = (
            (jax.ShapeDtypeStruct((width, 3 * group), F32),)
            + out_shape
            + (jax.ShapeDtypeStruct((8, width), F32),)
        )
        scratch = []
    return run(
        functools.partial(close_kernel, own, group, rows, split),
        [me],
        [dqkv, act, w, x, *os, *dbs, sums2, usum_a, usum_b],
        out_shape,
        scratch,
        30,
        10.5,
    )


def finish_kernel(vec, x, dh, part, near, far, out):
    da = part[...] + near[: part.shape[0], :].astype(F32) + far[...].astype(F32)
    xhat, rstd = normalise(x[...].astype(F32))
    out[...] = (dh[...] + norm_back(da, vec[0:1, :], xhat, rstd)).astype(BF)


def finish(vec, x, dh, part, near, far):
    return run(
        finish_kernel,
        [],
        [vec, x, dh, part, near, far],
        (jax.ShapeDtypeStruct(x.shape, BF),),
        [],
        8,
        3.0,
    )[0]


def share_kernel(own, group, place_ref, own_sum, got1, got2, got3, feed, *outs):
    me = place_ref[0]
    total = own_sum[:own, :]
    lines = own_sum[own:, :]
    for got in (got1, got2, got3):
        total = total + got[:own, :].astype(F32)
        lines = lines + got[own : own + 8, :].astype(F32) + got[own + 8 :, :].astype(F32)
    low = total.astype(BF)
    rows = [lines[0:1, i * group : (i + 1) * group] for i in range(4)]
    rows += [lines[1:2, i * group : (i + 1) * group] for i in range(2)]
    rows += [jnp.zeros((2, group), F32)]
    high, rest = split_low(jnp.concatenate(rows, 0))
    orders = ((0, 1, 2), (1, 0, 2), (1, 2, 0), (2, 1, 0))
    for k in range(4):
        outs[k][:8, :] = high
        outs[k][8:16, :] = rest
    for s in range(4):

        @pl.when(me == s)
        def _(s=s):
            for k in range(4):
                unit = orders[s][min(k, 2)]
                c = s ^ k
                outs[k][16 : 16 + own, :] = low[:, unit * group : (unit + 1) * group]
                outs[k][16 + own :, :] = feed[:, c * group : (c + 1) * group]

    outs[4][...] = low[:, 3 * group :]


def share(me, own_sum, arrived, feed):
    own, width = feed.shape[0] // 2, feed.shape[1]
    group = width // 4
    piece = jax.ShapeDtypeStruct((16 + 3 * own, group), BF)
    return run(
        functools.partial(share_kernel, own, group),
        [me],
        [own_sum, *arrived, feed],
        (piece,) * 4 + (jax.ShapeDtypeStruct((own, group), BF),),
        [],
        10,
        3.0,
    )


def settle_kernel(own, group, place_ref, *refs):
    pieces, out = refs[:4], refs[4]
    qkv_grad, up_grad, down_grad, out_grad, sums = refs[5:]
    me = place_ref[0]
    half = group // 2
    total = 0.0
    for piece in pieces:
        total = total + piece[:8, :].astype(F32) + piece[8:16, :].astype(F32)
    sums[...] = total
    out_grad[...] = out[...].astype(F32)
    for s in range(4):

        @pl.when(me == s)
        def _(s=s):
            for k in range(4):
                c = s ^ k
                if k < 3:
                    spot = k if s % 2 == 0 else 2 - k
                    qkv_grad[:, spot * group : (spot + 1) * group] = pieces[k][
                        16 : 16 + own, :
                    ].astype(F32)
                up = pieces[k][16 + own : 16 + 2 * own, :].astype(F32)
                for j in range(2):
                    start = (4 * j + c) * half
                    up_grad[:, start : start + half] = up[:, j * half : (j + 1) * half]
                down_grad[c * own : (c + 1) * own, :] = pieces[k][16 + 2 * own :, :].astype(F32)


def settle(me, pieces, out):
    own, group = out.shape
    return run(
        functools.partial(settle_kernel, own, group),
        [me],
        [*pieces, out],
        (
            jax.ShapeDtypeStruct((own, 3 * group), F32),
            jax.ShapeDtypeStruct((own, 4 * group), F32),
            jax.ShapeDtypeStruct((4 * own, group), F32),
            jax.ShapeDtypeStruct((own, group), F32),
            jax.ShapeDtypeStruct((8, group), F32),
        ),
        [],
        8,
        3.8,
    )


def body(
    frames_in,
    norm1_gain,
    norm1_bias,
    qkv_weight,
    query_bias,
    value_bias,
    out_weight,
    out_bias,
    norm2_gain,
    norm2_bias,
    up_weight,
    up_bias,
    down_weight,
    down_bias,
    cotangent,
):
    count = lax.axis_size("fsdp")
    q = count // GROUPS
    s = lax.axis_index("seq")
    f = lax.axis_index("fsdp")
    width = frames_in.shape[2]
    rows = frames_in.shape[0] * frames_in.shape[1]
    group = width // GROUPS
    own = qkv_weight.shape[0]
    hidden_all = up_weight.shape[1]
    hidden = hidden_all // GROUPS
    hid_own = down_weight.shape[0]
    ring = count == 8
    planes = count // 2 if ring else 1
    me = jnp.stack([s, f % 2, f // 2, f % GROUPS]).astype(jnp.int32)

    x = frames_in.reshape(rows, width)
    dy = cotangent.reshape(rows, width)

    vectors = jnp.concatenate(
        [
            norm1_gain,
            norm1_bias,
            query_bias,
            value_bias,
            out_bias,
            norm2_gain,
            norm2_bias,
            down_bias,
            up_bias,
        ]
    )
    lines = -(-vectors.shape[0] // width)
    padded = jnp.pad(vectors, (0, lines * width - vectors.shape[0])).reshape(lines, width)
    qkv_own = lax.dynamic_index_in_dim(
        qkv_weight.reshape(own, 3, GROUPS, group), s, 2, keepdims=False
    ).reshape(own, 3 * group)
    out_own = lax.dynamic_index_in_dim(
        out_weight.reshape(own, GROUPS, group), s, 1, keepdims=False
    )
    packed = jnp.concatenate([jnp.concatenate([qkv_own, out_own], 1), padded], 0)
    if ring:
        vec = None
        x_pieces = [x] + [seq_swap(x, k) for k in (1, 2, 3)]
        where, qkv_blocks = ring_gather(packed, count)
        pair = own_units(me, after(up_weight, *qkv_blocks[1:3]), down_weight)
        up_blocks = [lax.all_gather(pair, "fsdp", axis=0, tiled=True)]
        down_blocks = []
    else:
        where = jnp.zeros((8,), jnp.int32)
        x_pieces = seq_pieces(x)
        up_own = lax.dynamic_index_in_dim(
            up_weight.reshape(own, count, GROUPS, own), s, 2, keepdims=False
        ).reshape(own, hidden)
        down_own = lax.dynamic_slice_in_dim(down_weight, s * own, own, 0)
        first = lax.all_gather(packed, "fsdp", axis=0, tiled=False)
        qkv_blocks = [first[:, :own, : 3 * group].reshape(width, 3 * group)]
        spread = first[:, own:].reshape(count, lines * width).astype(F32)
        gain1, bias1, qb, vb, bo, gain2, bias2, bd = (
            spread[:, i * own : (i + 1) * own].reshape(width) for i in range(8)
        )
        bu = spread[:, 8 * own : 8 * own + hid_own].reshape(hidden_all)
        bias = jnp.concatenate(
            [
                lax.dynamic_slice_in_dim(qb, s * group, group),
                jnp.zeros((group,), F32),
                lax.dynamic_slice_in_dim(vb, s * group, group),
                jnp.zeros((group,), F32),
            ]
        )
        bu = lax.dynamic_index_in_dim(
            bu.reshape(count, GROUPS, own), s, 1, keepdims=False
        ).reshape(hidden)
        vec = jnp.stack([gain1, bias1, bias, bo, gain2, bias2, bd, bu])
        second = lax.all_gather(
            jnp.concatenate([up_own, out_weight, down_own], 0), "fsdp", axis=0, tiled=False
        )
        up_blocks = [second[:, :own].reshape(width, hidden)]
        out_blocks = [second[:, own : 2 * own].reshape(width, width)]
        down_blocks = [second[:, 2 * own :].reshape(hidden, width)]

    act1, queries, keys, values, k_turned, v_turned, w_qkv, w_col, vec, x_kept = project(
        where, me, x_pieces, qkv_blocks, vec, own, group
    )
    if ring:
        out_blocks = [w_col, seq_swap(w_col, 1), seq_swap(w_col, 2)]
    o2, o3, lse_b = attend(1, queries, keys, v_turned)
    far2, far3 = seq_swap(o2, 2), seq_swap(o3, 3)
    queries_a = after(queries, o2)
    if ring:
        out_blocks.append(seq_swap(after(out_blocks[2], o2), 1))
    o0, o1, lse_a = attend(0, queries_a, keys, v_turned)
    o_pieces = [o0, seq_swap(o1, 1), far2, far3]
    pieces = seq_pieces(after(dy, o0))
    h, act2, w_out = mix(where, me, vec, x, o_pieces, out_blocks, own, group)
    a_pieces = [act2, seq_swap(act2, 1), seq_swap(act2, 2)]
    g_a, du_a, part0, part1, usum_a, w_up, w_down = feed(
        where, vec, a_pieces[:2], pieces[:2], up_blocks, down_blocks, own
    )
    a_pieces.append(seq_swap(after(a_pieces[2], g_a), 1))
    near0 = seq_swap(part1, 1)
    g_b, du_b, part2, part3, usum_b, _, _ = feed(
        where, vec, a_pieces[2:], pieces[2:], [w_up], [w_down], own
    )
    near2 = seq_swap(part3, 1)
    far_sum = (part2 + near2.astype(F32)).astype(BF)
    far = seq_swap(far_sum, 2)

    du_late = after(du_b, far_sum)
    feed_parts = feed_grads(a_pieces, pieces, (g_a, g_b), (du_a, du_late), own)
    feed_total = fsdp_reduce(feed_parts)
    far = after(far, feed_parts)
    dh, db, sums2 = turn(me, vec, h, dy, part0, near0, far)
    db_pieces = [db, seq_swap(db, 1), seq_swap(db, 2)]
    y_parts = feed_out((g_a, after(g_b, db)), w_down)
    lse_a = after(lse_a, y_parts[0])
    back_a = back_first(me, queries, keys, values, k_turned, lse_a, db_pieces[:2], w_out)
    db_pieces.append(seq_swap(after(db_pieces[2], back_a[0]), 1))
    y_near = seq_swap(after(y_parts[2], back_a[0]), 1)
    y_sum = (y_parts[1] + y_near[rows:].astype(F32)).astype(BF)
    lse_b = after(lse_b, back_a[0])
    dqkv = back_second(
        me, queries, keys, values, k_turned, lse_b, w_out, back_a, db_pieces[2:]
    )
    y_far = seq_swap(after(y_sum, back_a[0]), 2)
    os = (o0, o1, o2, o3)
    closed = close(
        me, dqkv, act1, w_qkv, x_kept, os, db_pieces, sums2, usum_a, usum_b, own, planes
    )
    if ring:
        keep, give, part0, part2, sent = closed
        got = side_swap(give, count)
    else:
        grad_heads, part0, part2, sent, sums1 = closed
    near = seq_swap(sent, 1)
    far_sum = (part2 + near[rows:].astype(F32)).astype(BF)
    if ring:
        got = after(got, far_sum)
        own_sum, *sends = plane_parts(me, keep, got)
        arrived = plane_swaps(sends, count)
    far1 = seq_swap(far_sum, 2)
    layer_out = h + (y_parts[0] + y_near[:rows].astype(F32) + y_far.astype(F32)) + vec[6]
    layer_out = layer_out.astype(BF).reshape(frames_in.shape)
    input_grad = finish(vec, x, dh, part0, near, far1).reshape(frames_in.shape)
    if ring:
        *shares, out_block = share(me, own_sum, arrived, feed_total)
        shares = [shares[0]] + [seq_swap(shares[step], step) for step in (1, 2, 3)]
        out_block = to_owners(out_block, count, 0)
        grad_qkv, grad_up, grad_down, grad_out, vectors = settle(me, shares, out_block)
        vectors = vectors.reshape(16, own)
        g_gain1, g_bias1, g_query, g_value, g_outb, g_gain2, g_bias2, g_downb = (
            vectors[i] for i in range(8)
        )
        g_upb = vectors[8:12].reshape(hid_own)
    else:
        units = fsdp_reduce(grad_heads.reshape(count, own, 3 * group)).astype(BF)
        units = units.reshape(own, 3, group)
        order = jnp.array([[0, 1, 2], [1, 0, 2], [1, 2, 0], [2, 1, 0]], jnp.int32)[s]
        got = [lax.dynamic_index_in_dim(units, order[k], 1, keepdims=False) for k in range(3)]
        got = [got[0], seq_swap(got[1], 1), seq_swap(got[2], 2)]
        odd = s % 2 == 1
        grad_qkv = jnp.concatenate(
            [jnp.where(odd, got[2], got[0]), got[1], jnp.where(odd, got[0], got[2])], 1
        ).astype(F32)
        grad_up, grad_down = feed_total[:own].astype(F32), feed_total[own:]
        out_parts = out_grads(me, [o0, o1, o2, o3], db_pieces, own)
        grad_out = to_owners(fsdp_reduce(out_parts[0]).astype(BF), count, 0).astype(F32)
        grad_down = lax.all_to_all(
            grad_down, "seq", split_axis=1, concat_axis=0, tiled=True
        ).astype(F32)
        grad_up = lax.all_to_all(
            grad_up.astype(BF).reshape(own, GROUPS, q, own), "seq", split_axis=1, concat_axis=1
        )
        grad_up = grad_up.transpose(0, 2, 1, 3).reshape(own, hidden).astype(F32)

        def placed(values, size):
            return lax.dynamic_update_slice_in_dim(
                jnp.zeros((size,), F32), values, s * values.shape[0], 0
            ).reshape(count, size // count)

        sums = [
            sums1[0].reshape(count, own),
            sums1[1].reshape(count, own),
            placed(sums1[2, :group], width),
            placed(sums1[2, 2 * group : 3 * group], width),
            sums2[0].reshape(count, own),
            sums2[1].reshape(count, own),
            sums2[2].reshape(count, own),
            sums2[3].reshape(count, own),
            lax.dynamic_update_slice_in_dim(
                jnp.zeros((count, hid_own), F32),
                (usum_a[0] + usum_b[0]).reshape(count, own),
                s * own,
                1,
            ),
        ]
        total = lax.psum(fsdp_reduce(jnp.concatenate(sums, 1)), "seq")
        g_gain1, g_bias1, g_query, g_value, g_outb, g_gain2, g_bias2, g_downb = (
            total[i * own : (i + 1) * own] for i in range(8)
        )
        g_upb = total[8 * own :]

    return (
        layer_out,
        input_grad,
        g_gain1,
        g_bias1,
        grad_qkv,
        g_query,
        g_value,
        grad_out,
        g_outb,
        g_gain2,
        g_bias2,
        grad_up,
        g_upb,
        grad_down,
        g_downb,
    )


def solution(mesh):
    tokens = P("fsdp", "seq", None)
    vector = P("fsdp")
    matrix = P("fsdp", None)
    summed = P("fsdp", "seq")
    return jax.shard_map(
        body,
        mesh=mesh,
        in_specs=(
            tokens,
            vector,
            vector,
            matrix,
            vector,
            vector,
            matrix,
            vector,
            vector,
            vector,
            matrix,
            vector,
            matrix,
            vector,
            tokens,
        ),
        out_specs=(
            tokens,
            tokens,
            vector,
            vector,
            summed,
            vector,
            vector,
            summed,
            vector,
            vector,
            vector,
            summed,
            vector,
            summed,
            vector,
        ),
        check_vma=False,
    )
```

```python
import functools

import jax
import jax.numpy as jnp
from jax import lax
from jax.experimental import pallas as pl
from jax.experimental.pallas import tpu as pltpu
from jax.sharding import PartitionSpec as P

HD = 64
GROUPS = 4
epsilon = 1e-05
BF = jnp.bfloat16
F32 = jnp.float32


def dot(a, b):
    return jnp.dot(a, b, preferred_element_type=F32)


def dot_tn(a, b):
    return lax.dot_general(a, b, (((0,), (0,)), ((), ())), preferred_element_type=F32)


def dot_nt(a, b):
    return lax.dot_general(a, b, (((1,), (1,)), ((), ())), preferred_element_type=F32)


def seq_swap(value, step):
    return lax.ppermute(value, "seq", [(i, i ^ step) for i in range(GROUPS)])


def seq_pieces(value):
    near = seq_swap(value, 1)
    far = seq_swap(value, 2)
    return [value, near, far, seq_swap(far, 1)]


def fsdp_reduce(blocks):
    return lax.psum_scatter(blocks, "fsdp", scatter_dimension=0, tiled=False)


def side_swap(value, count):
    return lax.ppermute(value, "fsdp", [(i, i ^ 1) for i in range(count)])


def plane_swaps(parts, count):
    return [
        lax.ppermute(part, "fsdp", [(i, i ^ (2 * step)) for i in range(count)])
        for step, part in enumerate(parts, 1)
    ]


def add_all(own, arrived):
    for part in arrived:
        own = own + part.astype(F32)
    return own


def ring_order(count):
    return list(range(0, count, 2)) + list(range(count - 1, 0, -2))


def ring_gather(value, count):
    order = ring_order(count)
    ahead = [(order[i], order[(i + 1) % count]) for i in range(count)]
    back = [(b, a) for a, b in ahead]
    half = value.shape[0] // 32 * 16
    blocks, shifts = [value], [0]
    left = right = value
    for step in range(1, count // 2):
        left = lax.ppermute(left, "fsdp", ahead)
        right = lax.ppermute(right, "fsdp", back)
        blocks += [left, right]
        shifts += [-step, step]
    last = [lax.ppermute(left[:half], "fsdp", ahead), lax.ppermute(right[half:], "fsdp", back)]
    blocks.append(jnp.concatenate(last, 0))
    shifts.append(count // 2)
    spot = jnp.array([order.index(i) for i in range(count)], jnp.int32)[lax.axis_index("fsdp")]
    sources = jnp.array(order, jnp.int32)[(spot + jnp.array(shifts, jnp.int32)) % count]
    return sources, blocks


def after(value, *others):
    return lax.optimization_barrier((value,) + others)[0]


def to_groups(value, count):
    q = count // GROUPS
    pairs = []
    for s in range(GROUPS):
        for j in range(q):
            for t in range(GROUPS):
                pairs.append(((q * s + j) * GROUPS + t, (GROUPS * j + t) * GROUPS + s))
    return lax.ppermute(value, ("fsdp", "seq"), pairs)


def to_owners(value, count, step):
    q = count // GROUPS
    pairs = []
    for s in range(GROUPS):
        for j in range(q):
            for t in range(GROUPS):
                pairs.append(
                    ((GROUPS * j + t) * GROUPS + s, (q * s + j) * GROUPS + (t ^ step))
                )
    return lax.ppermute(value, ("fsdp", "seq"), pairs)


def normalise(values):
    center = values - jnp.mean(values, -1, keepdims=True)
    rstd = lax.rsqrt(jnp.mean(center * center, -1, keepdims=True) + epsilon)
    return center * rstd, rstd


def norm_back(grad, gain, xhat, rstd):
    e = grad * gain
    return rstd * (
        e - jnp.mean(e, -1, keepdims=True) - xhat * jnp.mean(e * xhat, -1, keepdims=True)
    )


def params(megabytes=26):
    return pltpu.CompilerParams(vmem_limit_bytes=megabytes * 2**20)


SMEM = pl.BlockSpec(memory_space=pltpu.SMEM)
VMEM = pl.BlockSpec(memory_space=pltpu.VMEM)
ANY = pl.BlockSpec(memory_space=pl.ANY)


def run(kernel, scalars, arrays, out_shape, scratch, megabytes, micros, direct=False):
    n_scalars, n_arrays, n_outs = len(scalars), len(arrays), len(out_shape)

    estimate = pl.CostEstimate(
        flops=int(micros * 10**9), bytes_accessed=2**20, transcendentals=0
    )
    if direct:
        return pl.pallas_call(
            kernel,
            out_shape=tuple(out_shape),
            in_specs=[SMEM] * n_scalars + [VMEM] * n_arrays,
            out_specs=(VMEM,) * n_outs,
            scratch_shapes=list(scratch),
            compiler_params=params(megabytes),
            cost_estimate=estimate,
        )(*scalars, *arrays)

    def wrapped(*refs):
        rest = refs[n_scalars + n_arrays :]
        outs, own = rest[:n_outs], rest[n_outs : n_outs + len(scratch)]
        held, sems = rest[n_outs + len(scratch) : -1], rest[-1]
        copies = [
            pltpu.make_async_copy(refs[n_scalars + i], held[i], sems.at[i])
            for i in range(n_arrays)
        ]
        for copy in copies:
            copy.start()
        for copy in copies:
            copy.wait()
        kernel(*refs[:n_scalars], *held, *outs, *own)

    return pl.pallas_call(
        wrapped,
        out_shape=tuple(out_shape),
        in_specs=[SMEM] * n_scalars + [ANY] * n_arrays,
        out_specs=(VMEM,) * n_outs,
        scratch_shapes=list(scratch)
        + [pltpu.VMEM(a.shape, a.dtype) for a in arrays]
        + [pltpu.SemaphoreType.DMA((n_arrays,))],
        compiler_params=params(megabytes),
        cost_estimate=estimate,
    )(*scalars, *arrays)


def lane_ids(width):
    return lax.broadcasted_iota(jnp.int32, (1, width), 1)


def collect_vectors(where, me, blocks, own, group, vec, table):
    count = len(blocks)
    width = count * own
    table[...] = jnp.zeros_like(table)
    for i, block in enumerate(blocks):
        pair = block[own : own + 2, :].astype(F32)
        table[0, pl.ds(where[i], 1), :] = pair[0:1]
        table[1, pl.ds(where[i], 1), :] = pair[1:2]
    lanes = lax.broadcasted_iota(jnp.int32, (count, width), 1)
    rows = lax.broadcasted_iota(jnp.int32, (count, width), 0)
    mine = (lanes >= rows * own) & (lanes < (rows + 1) * own)
    base = table[0]
    shifted_base = [base] + [pltpu.roll(base, k * own, 1) for k in range(1, count)]

    def whole(index, shifted=None):
        shifted = shifted or shifted_base
        picked = jnp.zeros((count, width), F32)
        for k in range(count):
            here = mine & (rows == (k + index) % count)
            picked = jnp.where(here, shifted[k], picked)
        return jnp.sum(picked, 0, keepdims=True)

    gain1, bias1, qb, vb, bo, gain2, bias2, bd = (whole(i) for i in range(8))
    lane = lane_ids(width)
    qb = pltpu.roll(qb, lax.rem(width - me * group, width), 1)
    vb = pltpu.roll(vb, lax.rem(width + 2 * group - me * group, width), 1)
    bias = jnp.where(lane < group, qb, 0.0)
    bias = jnp.where((lane >= 2 * group) & (lane < 3 * group), vb, bias)
    units = pltpu.roll(table[1], lax.rem(width - me * own, width), 1)
    shifted = [units] + [pltpu.roll(units, k * own, 1) for k in range(1, count)]
    bu = whole(0, shifted)
    for i, row in enumerate((gain1, bias1, bias, bo, gain2, bias2, bd, bu)):
        vec[i : i + 1, :] = row


def units_kernel(own, place_ref, up, down, pair):
    me = place_ref[0]
    count = up.shape[1] // (4 * own)
    for s in range(4):

        @pl.when(me == s)
        def _(s=s):
            for f in range(count):
                start = (4 * f + s) * own
                pair[:own, f * own : (f + 1) * own] = up[:, start : start + own]
            pair[own:, :] = down[s * own : (s + 1) * own, :]


def own_units(me, up, down):
    own, width = up.shape[0], down.shape[1]
    return run(
        functools.partial(units_kernel, own),
        [me],
        [up, down],
        (jax.ShapeDtypeStruct((2 * own, width), BF),),
        [],
        8,
        3.0,
    )[0]


def project_kernel(ring, own, group, rows, *refs):
    where, place_ref = refs[0], refs[1]
    x_refs = refs[2:6]
    n_blocks = 8 if ring else 1
    blocks = refs[6 : 6 + n_blocks]
    rest = refs[6 + n_blocks :]
    if not ring:
        vec_in, rest = rest[0], rest[1:]
    act, queries, keys, values, k_turned, v_turned, w, w_col, vec, kept, table = rest
    me = place_ref[0]
    heads = group // HD
    if ring:
        collect_vectors(where, me, blocks, own, group, vec, table)
    else:
        vec[...] = vec_in[...]
    if ring:
        for i, block in enumerate(blocks):
            start = pl.multiple_of(where[i] * own, own)
            w[pl.ds(start, own), :] = block[:own, : 3 * group]
            w_col[pl.ds(start, own), :] = block[:own, 3 * group :]
    else:
        w[...] = blocks[0][...]
        w_col[...] = jnp.zeros_like(w_col)
    gain, shift, bias = vec[0:1, :], vec[1:2, :], vec[2:3, : 3 * group]
    for k in range(4):
        here = slice(k * rows, (k + 1) * rows)
        values_in = x_refs[k][...]
        kept[here, :] = values_in
        xhat, _ = normalise(values_in.astype(F32))
        block = (xhat * gain + shift).astype(BF)
        act[here, :] = block
        qkv = (dot(block, w[...]) + bias).astype(BF)
        queries[here, :] = qkv[:, :group] * jnp.asarray(HD ** (-0.5), BF)
        for head in range(heads):
            keys[head, here, :] = qkv[:, group + head * HD : group + (head + 1) * HD]
            values[head, here, :] = qkv[:, 2 * group + head * HD : 2 * group + (head + 1) * HD]
        k_turned[:, here] = qkv[:, group : 2 * group].T
        v_turned[:, here] = qkv[:, 2 * group : 3 * group].T


def project(where, me, pieces, blocks, vec, own, group):
    rows, width = pieces[0].shape
    frames = 4 * rows
    heads = group // HD
    ring = len(blocks) > 1
    out_shape = (
        jax.ShapeDtypeStruct((frames, width), BF),
        jax.ShapeDtypeStruct((frames, group), BF),
        jax.ShapeDtypeStruct((heads, frames, HD), BF),
        jax.ShapeDtypeStruct((heads, frames, HD), BF),
        jax.ShapeDtypeStruct((group, frames), BF),
        jax.ShapeDtypeStruct((group, frames), BF),
        jax.ShapeDtypeStruct((width, 3 * group), BF),
        jax.ShapeDtypeStruct((width, group), BF),
        jax.ShapeDtypeStruct((8, width), F32),
        jax.ShapeDtypeStruct((frames, width), BF),
    )
    args = [where, me, *pieces, *blocks] + ([] if ring else [vec])
    return run(
        functools.partial(project_kernel, ring, own, group, rows),
        args[:2],
        args[2:],
        out_shape,
        [pltpu.VMEM((2, 8, width), F32)],
        16,
        9.0,
        direct=True,
    )


def attend_kernel(group, rows, part, queries, keys, v_turned, first, second, lse):
    heads = group // HD
    lse[...] = jnp.zeros_like(lse)
    for t, out in enumerate((first, second)):
        turned = []
        for head in range(heads):
            start = (2 * part + t) * rows
            query = queries[start : start + rows, head * HD : (head + 1) * HD]
            scores = dot_nt(keys[head], query)
            top = jnp.max(scores, 0, keepdims=True)
            e = jnp.exp(scores - top)
            total = jnp.sum(e, 0, keepdims=True)
            lse[head : head + 1, t * rows : (t + 1) * rows] = top + jnp.log(total)
            p = (e * (1.0 / total)).astype(BF)
            turned.append(dot(v_turned[head * HD : (head + 1) * HD, :], p))
        out[...] = jnp.concatenate(turned, 0).T.astype(BF)


def attend(part, queries, keys, v_turned):
    frames, group = queries.shape
    rows = frames // 4
    return run(
        functools.partial(attend_kernel, group, rows, part),
        [],
        [queries, keys, v_turned],
        (
            jax.ShapeDtypeStruct((rows, group), BF),
            jax.ShapeDtypeStruct((rows, group), BF),
            jax.ShapeDtypeStruct((8, 2 * rows), F32),
        ),
        [],
        10,
        7.5,
    )


def mix_kernel(own, group, rows, *refs):
    where, place_ref, vec, x = refs[:4]
    o_refs = refs[4:8]
    blocks, (h, act, w) = refs[8:-3], refs[-3:]
    me = place_ref[0]
    if len(blocks) == 1:
        w[...] = blocks[0][...]
    else:
        for k, block in enumerate(blocks):
            for c in range(4):

                @pl.when((me ^ k) == c)
                def _(block=block, c=c):
                    w[:, c * group : (c + 1) * group] = block[...]

    total = x[...].astype(F32) + vec[3:4, :]
    for k in range(4):
        start = pl.multiple_of((me ^ k) * group, group)
        total = total + dot(o_refs[k][:rows, :], w[pl.ds(start, group), :])
    h[...] = total
    xhat, _ = normalise(total)
    act[...] = (xhat * vec[4:5, :] + vec[5:6, :]).astype(BF)


def mix(where, me, vec, x, pieces, blocks, own, group):
    rows, width = x.shape
    args = [where, me, vec, x, *pieces, *blocks]
    return run(
        functools.partial(mix_kernel, own, group, rows),
        args[:2],
        args[2:],
        (
            jax.ShapeDtypeStruct((rows, width), F32),
            jax.ShapeDtypeStruct((rows, width), BF),
            jax.ShapeDtypeStruct((width, width), BF),
        ),
        [],
        10,
        6.0,
    )


def feed_kernel(n_up, n_down, own, rows, *refs):
    where, vec, a0, a1, dy0, dy1 = refs[:6]
    ups = refs[6 : 6 + n_up]
    downs = refs[6 + n_up : 6 + n_up + n_down]
    g, du, first, second, total, w_up, w_down = refs[6 + n_up + n_down :]
    if n_down:
        w_up[...] = ups[0][...]
        w_down[...] = downs[0][...]
    elif len(ups) == 1:
        for i in range(w_up.shape[0] // own):
            here = slice(i * own, (i + 1) * own)
            w_up[here, :] = ups[0][2 * i * own : (2 * i + 1) * own, :]
            w_down[here, :] = ups[0][(2 * i + 1) * own : (2 * i + 2) * own, :]
    else:
        for i, block in enumerate(ups):
            start = pl.multiple_of(where[i] * own, own)
            skip = block.shape[0] - 2 * own
            w_up[pl.ds(start, own), :] = block[skip : skip + own, :]
            w_down[pl.ds(start, own), :] = block[skip + own :, :]
    bias = vec[7:8, :]
    total[...] = jnp.zeros_like(total)
    chunk = rows // 2
    for part, (a, dy, out) in enumerate(((a0, dy0, first), (a1, dy1, second))):
        for c in range(2):
            here = slice(c * chunk, (c + 1) * chunk)
            there = slice(part * rows + c * chunk, part * rows + (c + 1) * chunk)
            u = dot(a[here, :], w_up[...]) + bias
            cdf = 0.5 * (1.0 + lax.erf(u * (0.5**0.5)))
            pdf = jnp.exp(-0.5 * u * u) * ((2.0 * jnp.pi) ** (-0.5))
            g[there, :] = (u * cdf).astype(BF)
            grad = (dot_nt(dy[here, :], w_down[...]) * (cdf + u * pdf)).astype(BF)
            du[there, :] = grad
            total[0:1, :] += jnp.sum(grad.astype(F32), 0, keepdims=True)
            out[here, :] = dot_nt(grad, w_up[...]).astype(out.dtype)


def feed(where, vec, acts, dys, ups, downs, own):
    rows, width = acts[0].shape
    hidden = ups[0].shape[1]
    assert width == hidden
    args = [where, vec, *acts, *dys, *ups, *downs]
    return run(
        functools.partial(feed_kernel, len(ups), len(downs), own, rows),
        args[:1],
        args[1:],
        (
            jax.ShapeDtypeStruct((2 * rows, hidden), BF),
            jax.ShapeDtypeStruct((2 * rows, hidden), BF),
            jax.ShapeDtypeStruct((rows, width), F32),
            jax.ShapeDtypeStruct((rows, width), BF),
            jax.ShapeDtypeStruct((8, hidden), F32),
            jax.ShapeDtypeStruct((width, hidden), BF),
            jax.ShapeDtypeStruct((hidden, width), BF),
        ),
        [],
        18,
        8.2,
    )


def feed_out_kernel(rows, g_a, g_b, w, first, third, sent):
    for k in (1, 3, 0, 2):
        here = slice((k % 2) * rows, (k % 2 + 1) * rows)
        part = dot((g_a if k < 2 else g_b)[here, :], w[...])
        if k == 0:
            first[...] = part
        elif k == 2:
            third[...] = part
        else:
            sent[(k // 2) * rows : (k // 2 + 1) * rows, :] = part.astype(BF)


def feed_out(gs, w):
    rows = gs[0].shape[0] // 2
    width = w.shape[1]
    return run(
        functools.partial(feed_out_kernel, rows),
        [],
        [*gs, w],
        (
            jax.ShapeDtypeStruct((rows, width), F32),
            jax.ShapeDtypeStruct((rows, width), F32),
            jax.ShapeDtypeStruct((2 * rows, width), BF),
        ),
        [],
        10,
        3.0,
    )


def turn_kernel(*refs):
    vec, h, dy, part, near, far = refs[1:7]
    dh, db, sums = refs[7:]
    da = part[...] + near[...].astype(F32) + far[...].astype(F32)
    xhat, rstd = normalise(h[...])
    cot = dy[...].astype(F32)
    grad = cot + norm_back(da, vec[4:5, :], xhat, rstd)
    dh[...] = grad
    low = grad.astype(BF)
    db[...] = low
    sums[...] = jnp.zeros_like(sums)
    sums[0:1, :] = jnp.sum(low.astype(F32), 0, keepdims=True)
    sums[1:2, :] = jnp.sum(da * xhat, 0, keepdims=True)
    sums[2:3, :] = jnp.sum(da, 0, keepdims=True)
    sums[3:4, :] = jnp.sum(cot, 0, keepdims=True)


def turn(me, vec, h, dy, part, near, far):
    rows, width = h.shape
    return run(
        turn_kernel,
        [me],
        [vec, h, dy, part, near, far],
        (
            jax.ShapeDtypeStruct((rows, width), F32),
            jax.ShapeDtypeStruct((rows, width), BF),
            jax.ShapeDtypeStruct((8, width), F32),
        ),
        [],
        10,
        3.0,
    )


def back_tiles(me, group, rows, part, qkv, lse, db_refs, w, dk, dv, dq, skip):
    queries, keys, values, k_turned = qkv
    heads = group // HD
    for t in range(2):
        start = (2 * part + t) * rows
        turned = []
        w_own = w[pl.ds(pl.multiple_of(me * group, group), group), :]
        d_all = dot_nt(db_refs[t][...], w_own).astype(BF)
        for head in range(heads):
            here = slice(head * HD, (head + 1) * HD)
            query = queries[start : start + rows, here]
            d_out = d_all[:, here]
            scores = dot_nt(keys[head], query)
            p = jnp.exp(scores - lse[head : head + 1, t * rows : (t + 1) * rows])
            dv[head] += dot(p.astype(BF), d_out)
            dp = dot_nt(values[head], d_out)
            inner = jnp.sum(p * dp, 0, keepdims=True)
            ds = (p * (dp - inner)).astype(BF)
            dk[head] += dot(ds, query)
            turned.append(dot(k_turned[here, :], ds))
        dq[skip + t * rows : skip + (t + 1) * rows, :group] = (
            jnp.concatenate(turned, 0).T * HD ** (-0.5)
        ).astype(BF)


def back_first_kernel(group, rows, place_ref, *refs):
    qkv, (lse, db0, db1, w, dq, dk, dv) = refs[:4], refs[4:]
    dk[...] = jnp.zeros_like(dk)
    dv[...] = jnp.zeros_like(dv)
    back_tiles(place_ref[0], group, rows, 0, qkv, lse, (db0, db1), w, dk, dv, dq, 0)


def back_first(me, queries, keys, values, k_turned, lse, dbs, w):
    frames, group = queries.shape
    heads = group // HD
    total = jax.ShapeDtypeStruct((heads, frames, HD), F32)
    return run(
        functools.partial(back_first_kernel, group, frames // 4),
        [me],
        [queries, keys, values, k_turned, lse, *dbs, w],
        (jax.ShapeDtypeStruct((frames // 2, group), BF), total, total),
        [],
        18,
        12.0,
    )


def back_second_kernel(group, rows, place_ref, *refs):
    qkv, (lse, w, dq_first, dk_first, dv_first, db2, db3) = refs[:4], refs[4:11]
    dqkv, dk, dv = refs[11:]
    heads = group // HD
    dk[...] = dk_first[...]
    dv[...] = dv_first[...]
    dqkv[: 2 * rows, :group] = dq_first[...]
    dbs = (db2, db3)
    back_tiles(place_ref[0], group, rows, 1, qkv, lse, dbs, w, dk, dv, dqkv, 2 * rows)
    dqkv[:, group : 2 * group] = jnp.concatenate([dk[i] for i in range(heads)], 1).astype(BF)
    dqkv[:, 2 * group :] = jnp.concatenate([dv[i] for i in range(heads)], 1).astype(BF)


def back_second(me, queries, keys, values, k_turned, lse, w, first, dbs):
    frames, group = queries.shape
    heads = group // HD
    return run(
        functools.partial(back_second_kernel, group, frames // 4),
        [me],
        [queries, keys, values, k_turned, lse, w, *first, *dbs],
        (jax.ShapeDtypeStruct((frames, 3 * group), BF),),
        [pltpu.VMEM((heads, frames, HD), F32), pltpu.VMEM((heads, frames, HD), F32)],
        20,
        12.0,
    )[0]


def feed_grads_kernel(own, rows, *refs):
    acts, dys = refs[:4], refs[4:8]
    g_a, g_b, du_a, du_b = refs[8:12]
    out = refs[12]
    up, down = 0.0, 0.0
    for k in range(4):
        here = slice((k % 2) * rows, (k % 2 + 1) * rows)
        up = up + dot_tn(acts[k][...], (du_a if k < 2 else du_b)[here, :])
    for f in range(out.shape[0]):
        out[f, :own, :] = up[f * own : (f + 1) * own, :].astype(BF)
    for k in range(4):
        here = slice((k % 2) * rows, (k % 2 + 1) * rows)
        down = down + dot_tn((g_a if k < 2 else g_b)[here, :], dys[k][...])
    for f in range(out.shape[0]):
        out[f, own:, :] = down[f * own : (f + 1) * own, :].astype(BF)


def feed_grads(acts, dys, gs, dus, own):
    rows, width = acts[0].shape
    return run(
        functools.partial(feed_grads_kernel, own, rows),
        [],
        [*acts, *dys, *gs, *dus],
        (jax.ShapeDtypeStruct((width // own, 2 * own, width), BF),),
        [],
        20,
        9.0,
    )[0]


def out_grads_kernel(own, group, *refs):
    o_refs, db_refs, blocks = refs[1:5], refs[5:9], refs[9]
    total = 0.0
    for k in range(4):
        total = total + dot_tn(o_refs[k][...], db_refs[k][...])
    for j in range(group // own):
        for t in range(4):
            blocks[j * 4 + t] = total[j * own : (j + 1) * own, t * group : (t + 1) * group]


def out_grads(me, os, dbs, own):
    group = os[0].shape[1]
    return run(
        functools.partial(out_grads_kernel, own, group),
        [me],
        [*os, *dbs],
        (jax.ShapeDtypeStruct((group // own * 4, own, group), F32),),
        [],
        12,
        3.0,
    )


def plane_kernel(own, place_ref, keep, got, *outs):
    plane = place_ref[2]
    for step, out in enumerate(outs):
        z = plane ^ step
        total = keep[z, :own, :] + got[z, :own, :].astype(F32)
        lines = keep[z, own:, :] + got[z, own : own + 8, :].astype(F32)
        lines = lines + got[z, own + 8 :, :].astype(F32)
        if step == 0:
            out[:own, :] = total
            out[own:, :] = lines
        else:
            out[:own, :] = total.astype(BF)
            high, low = split_low(lines)
            out[own : own + 8, :] = high
            out[own + 8 :, :] = low


def plane_parts(me, keep, got):
    planes, height, width = keep.shape
    out_shape = [jax.ShapeDtypeStruct((height, width), F32)]
    out_shape += [jax.ShapeDtypeStruct((height + 8, width), BF)] * (planes - 1)
    return run(
        functools.partial(plane_kernel, height - 8),
        [me],
        [keep, got],
        tuple(out_shape),
        [],
        12,
        2.2,
    )


def split_low(value):
    high = value.astype(BF)
    return high, (value - high.astype(F32)).astype(BF)


def close_kernel(own, group, rows, split, place_ref, dqkv, act, w, x, *refs):
    o_refs, db_refs = refs[:4], refs[4:8]
    sums2, usum_a, usum_b = refs[8:11]
    if split:
        keep, give, first, third, sent, table, lines, grads = refs[11:]
    else:
        grads, first, third, sent, sums = refs[11:]
    width = w.shape[0]
    gain_sum, shift_sum = 0.0, 0.0
    for k in (1, 3, 0, 2):
        part = dot_nt(dqkv[k * rows : (k + 1) * rows, :], w[...])
        xhat, _ = normalise(x[k * rows : (k + 1) * rows, :].astype(F32))
        gain_sum = gain_sum + jnp.sum(part * xhat, 0, keepdims=True)
        shift_sum = shift_sum + jnp.sum(part, 0, keepdims=True)
        if k == 0:
            first[...] = part
        elif k == 2:
            third[...] = part
        else:
            sent[(k // 2) * rows : (k // 2 + 1) * rows, :] = part.astype(BF)
    dsum = jnp.sum(dqkv[...].astype(F32), 0, keepdims=True)
    if not split:
        sums[...] = jnp.zeros_like(sums)
        sums[0:1, :] = gain_sum
        sums[1:2, :] = shift_sum
        sums[2:3, : 3 * group] = dsum
        grads[...] = dot_tn(act[...], dqkv[...])
        return
    me, side = place_ref[0], place_ref[1]
    out = 0.0
    for k in range(4):
        out = out + dot_tn(o_refs[k][...], db_refs[k][...])
    for j in range(2):
        for t in range(4):
            start = (j * 4 + t) * own
            grads[start : start + own, 3 * group :] = out[
                j * own : (j + 1) * own, t * group : (t + 1) * group
            ]
    grads[:, : 3 * group] = dot_tn(act[...], dqkv[...])
    count = width // own
    lane = lane_ids(width)
    table[0:1, :] = gain_sum
    table[1:2, :] = shift_sum
    table[3:4, :] = jnp.zeros((1, width), F32)
    table[3:4, : 3 * group] = dsum
    spread = table[3:4, :]
    query = jnp.where(lane < group, spread, 0.0)
    value = jnp.where(lane < group, pltpu.roll(spread, 2 * group, 1), 0.0)
    table[2:3, :] = pltpu.roll(query, me * group, 1)
    table[3:4, :] = pltpu.roll(value, me * group, 1)
    table[4:8, :] = sums2[0:4, :]
    base = table[...]
    shifted = [base] + [pltpu.roll(base, k * own, 1) for k in range(1, count)]
    lanes = lax.broadcasted_iota(jnp.int32, (count, width), 1)
    ids = lax.broadcasted_iota(jnp.int32, (count, width), 0)
    mine = (lanes >= ids * own) & (lanes < (ids + 1) * own)
    units = pltpu.roll(usum_a[0:1, :] + usum_b[0:1, :], me * own, 1)
    inside = (lane >= me * own) & (lane < (me + 1) * own)
    for f in range(count):
        picked = jnp.zeros((count, width), F32)
        for k in range(count):
            picked = jnp.where(mine & (ids == (f + k) % count), shifted[k], picked)
        lines[f, 0:1, :] = jnp.sum(picked, 0, keepdims=True)
        turned = units if f == 0 else pltpu.roll(units, width - f * own, 1)
        lines[f, 1:2, :] = jnp.where(inside, turned, 0.0)
    for z in range(count // 2):
        mine_f, other = 2 * z + side, 2 * z + 1 - side
        keep[z, :own, :] = grads[pl.ds(pl.multiple_of(mine_f * own, own), own), :]
        keep[z, own:, :] = lines[mine_f]
        rest = grads[pl.ds(pl.multiple_of(other * own, own), own), :]
        give[z, :own, :] = rest.astype(BF)
        high, low = split_low(lines[other])
        give[z, own : own + 8, :] = high
        give[z, own + 8 :, :] = low


def close(me, dqkv, act, w, x, os, dbs, sums2, usum_a, usum_b, own, planes):
    rows, width = x.shape[0] // 4, x.shape[1]
    group = width // 4
    split = planes > 1
    out_shape = (
        jax.ShapeDtypeStruct((rows, width), F32),
        jax.ShapeDtypeStruct((rows, width), F32),
        jax.ShapeDtypeStruct((2 * rows, width), BF),
    )
    if split:
        out_shape = (
            jax.ShapeDtypeStruct((planes, own + 8, width), F32),
            jax.ShapeDtypeStruct((planes, own + 16, width), BF),
        ) + out_shape
        scratch = [
            pltpu.VMEM((8, width), F32),
            pltpu.VMEM((2 * planes, 8, width), F32),
            pltpu.VMEM((width, width), F32),
        ]
    else:
        out_shape = (
            (jax.ShapeDtypeStruct((width, 3 * group), F32),)
            + out_shape
            + (jax.ShapeDtypeStruct((8, width), F32),)
        )
        scratch = []
    return run(
        functools.partial(close_kernel, own, group, rows, split),
        [me],
        [dqkv, act, w, x, *os, *dbs, sums2, usum_a, usum_b],
        out_shape,
        scratch,
        30,
        10.5,
    )


def finish_kernel(vec, x, dh, part, near, far, out):
    da = part[...] + near[: part.shape[0], :].astype(F32) + far[...].astype(F32)
    xhat, rstd = normalise(x[...].astype(F32))
    out[...] = (dh[...] + norm_back(da, vec[0:1, :], xhat, rstd)).astype(BF)


def finish(vec, x, dh, part, near, far):
    return run(
        finish_kernel,
        [],
        [vec, x, dh, part, near, far],
        (jax.ShapeDtypeStruct(x.shape, BF),),
        [],
        8,
        3.0,
    )[0]


def share_kernel(own, group, place_ref, own_sum, got1, got2, got3, feed, *outs):
    me = place_ref[0]
    total = own_sum[:own, :]
    lines = own_sum[own:, :]
    for got in (got1, got2, got3):
        total = total + got[:own, :].astype(F32)
        lines = lines + got[own : own + 8, :].astype(F32) + got[own + 8 :, :].astype(F32)
    low = total.astype(BF)
    rows = [lines[0:1, i * group : (i + 1) * group] for i in range(4)]
    rows += [lines[1:2, i * group : (i + 1) * group] for i in range(2)]
    rows += [jnp.zeros((2, group), F32)]
    high, rest = split_low(jnp.concatenate(rows, 0))
    orders = ((0, 1, 2), (1, 0, 2), (1, 2, 0), (2, 1, 0))
    for k in range(4):
        outs[k][:8, :] = high
        outs[k][8:16, :] = rest
    for s in range(4):

        @pl.when(me == s)
        def _(s=s):
            for k in range(4):
                unit = orders[s][min(k, 2)]
                c = s ^ k
                outs[k][16 : 16 + own, :] = low[:, unit * group : (unit + 1) * group]
                outs[k][16 + own :, :] = feed[:, c * group : (c + 1) * group]

    outs[4][...] = low[:, 3 * group :]


def share(me, own_sum, arrived, feed):
    own, width = feed.shape[0] // 2, feed.shape[1]
    group = width // 4
    piece = jax.ShapeDtypeStruct((16 + 3 * own, group), BF)
    return run(
        functools.partial(share_kernel, own, group),
        [me],
        [own_sum, *arrived, feed],
        (piece,) * 4 + (jax.ShapeDtypeStruct((own, group), BF),),
        [],
        10,
        3.0,
    )


def settle_kernel(own, group, place_ref, *refs):
    pieces, out = refs[:4], refs[4]
    qkv_grad, up_grad, down_grad, out_grad, sums = refs[5:]
    me = place_ref[0]
    half = group // 2
    total = 0.0
    for piece in pieces:
        total = total + piece[:8, :].astype(F32) + piece[8:16, :].astype(F32)
    sums[...] = total
    out_grad[...] = out[...].astype(F32)
    for s in range(4):

        @pl.when(me == s)
        def _(s=s):
            for k in range(4):
                c = s ^ k
                if k < 3:
                    spot = k if s % 2 == 0 else 2 - k
                    qkv_grad[:, spot * group : (spot + 1) * group] = pieces[k][
                        16 : 16 + own, :
                    ].astype(F32)
                up = pieces[k][16 + own : 16 + 2 * own, :].astype(F32)
                for j in range(2):
                    start = (4 * j + c) * half
                    up_grad[:, start : start + half] = up[:, j * half : (j + 1) * half]
                down_grad[c * own : (c + 1) * own, :] = pieces[k][16 + 2 * own :, :].astype(F32)


def settle(me, pieces, out):
    own, group = out.shape
    return run(
        functools.partial(settle_kernel, own, group),
        [me],
        [*pieces, out],
        (
            jax.ShapeDtypeStruct((own, 3 * group), F32),
            jax.ShapeDtypeStruct((own, 4 * group), F32),
            jax.ShapeDtypeStruct((4 * own, group), F32),
            jax.ShapeDtypeStruct((own, group), F32),
            jax.ShapeDtypeStruct((8, group), F32),
        ),
        [],
        8,
        3.8,
    )


def body(
    frames_in,
    norm1_gain,
    norm1_bias,
    qkv_weight,
    query_bias,
    value_bias,
    out_weight,
    out_bias,
    norm2_gain,
    norm2_bias,
    up_weight,
    up_bias,
    down_weight,
    down_bias,
    cotangent,
):
    count = lax.axis_size("fsdp")
    q = count // GROUPS
    s = lax.axis_index("seq")
    f = lax.axis_index("fsdp")
    width = frames_in.shape[2]
    rows = frames_in.shape[0] * frames_in.shape[1]
    group = width // GROUPS
    own = qkv_weight.shape[0]
    hidden_all = up_weight.shape[1]
    hidden = hidden_all // GROUPS
    hid_own = down_weight.shape[0]
    ring = count == 8
    planes = count // 2 if ring else 1
    me = jnp.stack([s, f % 2, f // 2, f % GROUPS]).astype(jnp.int32)

    x = frames_in.reshape(rows, width)
    dy = cotangent.reshape(rows, width)

    vectors = jnp.concatenate(
        [
            norm1_gain,
            norm1_bias,
            query_bias,
            value_bias,
            out_bias,
            norm2_gain,
            norm2_bias,
            down_bias,
            up_bias,
        ]
    )
    lines = -(-vectors.shape[0] // width)
    padded = jnp.pad(vectors, (0, lines * width - vectors.shape[0])).reshape(lines, width)
    qkv_own = lax.dynamic_index_in_dim(
        qkv_weight.reshape(own, 3, GROUPS, group), s, 2, keepdims=False
    ).reshape(own, 3 * group)
    out_own = lax.dynamic_index_in_dim(
        out_weight.reshape(own, GROUPS, group), s, 1, keepdims=False
    )
    packed = jnp.concatenate([jnp.concatenate([qkv_own, out_own], 1), padded], 0)
    if ring:
        vec = None
        x_pieces = [x] + [seq_swap(x, k) for k in (1, 2, 3)]
        where, qkv_blocks = ring_gather(packed, count)
        pair = own_units(me, after(up_weight, *qkv_blocks[1:3]), down_weight)
        up_blocks = [lax.all_gather(pair, "fsdp", axis=0, tiled=True)]
        down_blocks = []
    else:
        where = jnp.zeros((8,), jnp.int32)
        x_pieces = seq_pieces(x)
        up_own = lax.dynamic_index_in_dim(
            up_weight.reshape(own, count, GROUPS, own), s, 2, keepdims=False
        ).reshape(own, hidden)
        down_own = lax.dynamic_slice_in_dim(down_weight, s * own, own, 0)
        first = lax.all_gather(packed, "fsdp", axis=0, tiled=False)
        qkv_blocks = [first[:, :own, : 3 * group].reshape(width, 3 * group)]
        spread = first[:, own:].reshape(count, lines * width).astype(F32)
        gain1, bias1, qb, vb, bo, gain2, bias2, bd = (
            spread[:, i * own : (i + 1) * own].reshape(width) for i in range(8)
        )
        bu = spread[:, 8 * own : 8 * own + hid_own].reshape(hidden_all)
        bias = jnp.concatenate(
            [
                lax.dynamic_slice_in_dim(qb, s * group, group),
                jnp.zeros((group,), F32),
                lax.dynamic_slice_in_dim(vb, s * group, group),
                jnp.zeros((group,), F32),
            ]
        )
        bu = lax.dynamic_index_in_dim(
            bu.reshape(count, GROUPS, own), s, 1, keepdims=False
        ).reshape(hidden)
        vec = jnp.stack([gain1, bias1, bias, bo, gain2, bias2, bd, bu])
        second = lax.all_gather(
            jnp.concatenate([up_own, out_weight, down_own], 0), "fsdp", axis=0, tiled=False
        )
        up_blocks = [second[:, :own].reshape(width, hidden)]
        out_blocks = [second[:, own : 2 * own].reshape(width, width)]
        down_blocks = [second[:, 2 * own :].reshape(hidden, width)]

    act1, queries, keys, values, k_turned, v_turned, w_qkv, w_col, vec, x_kept = project(
        where, me, x_pieces, qkv_blocks, vec, own, group
    )
    if ring:
        out_blocks = [w_col, seq_swap(w_col, 1), seq_swap(w_col, 2)]
    o2, o3, lse_b = attend(1, queries, keys, v_turned)
    far2, far3 = seq_swap(o2, 2), seq_swap(o3, 3)
    queries_a = after(queries, o2)
    o0, o1, lse_a = attend(0, queries_a, keys, v_turned)
    if ring:
        out_blocks.append(seq_swap(after(out_blocks[2], o0), 1))
    o_pieces = [o0, seq_swap(o1, 1), far2, far3]
    pieces = seq_pieces(after(dy, o0))
    h, act2, w_out = mix(where, me, vec, x, o_pieces, out_blocks, own, group)
    a_pieces = [act2, seq_swap(act2, 1), seq_swap(act2, 2)]
    g_a, du_a, part0, part1, usum_a, w_up, w_down = feed(
        where, vec, a_pieces[:2], pieces[:2], up_blocks, down_blocks, own
    )
    a_pieces.append(seq_swap(after(a_pieces[2], g_a), 1))
    near0 = seq_swap(part1, 1)
    g_b, du_b, part2, part3, usum_b, _, _ = feed(
        where, vec, a_pieces[2:], pieces[2:], [w_up], [w_down], own
    )
    near2 = seq_swap(part3, 1)
    far_sum = (part2 + near2.astype(F32)).astype(BF)
    far = seq_swap(far_sum, 2)

    du_late = after(du_b, far_sum)
    feed_parts = feed_grads(a_pieces, pieces, (g_a, g_b), (du_a, du_late), own)
    feed_total = fsdp_reduce(feed_parts)
    far = after(far, feed_parts)
    dh, db, sums2 = turn(me, vec, h, dy, part0, near0, far)
    db_pieces = [db, seq_swap(db, 1), seq_swap(db, 2)]
    back_a = back_first(me, queries, keys, values, k_turned, lse_a, db_pieces[:2], w_out)
    db_pieces.append(seq_swap(after(db_pieces[2], back_a[0]), 1))
    lse_b = after(lse_b, back_a[0])
    dqkv = back_second(
        me, queries, keys, values, k_turned, lse_b, w_out, back_a, db_pieces[2:]
    )
    os = (o0, o1, o2, o3)
    closed = close(
        me, dqkv, act1, w_qkv, x_kept, os, db_pieces, sums2, usum_a, usum_b, own, planes
    )
    if ring:
        keep, give, part0, part2, sent = closed
        got = side_swap(give, count)
    else:
        grad_heads, part0, part2, sent, sums1 = closed
    near = seq_swap(sent, 1)
    y_parts = feed_out((g_a, after(g_b, sent)), w_down)
    y_near = seq_swap(y_parts[2], 1)
    y_sum = (y_parts[1] + y_near[rows:].astype(F32)).astype(BF)
    far_sum = (part2 + near[rows:].astype(F32)).astype(BF)
    if ring:
        got = after(got, far_sum)
        own_sum, *sends = plane_parts(me, keep, got)
        arrived = plane_swaps(sends, count)
    far1 = seq_swap(far_sum, 2)
    y_far = seq_swap(after(y_sum, far_sum), 2)
    layer_out = h + (y_parts[0] + y_near[:rows].astype(F32) + y_far.astype(F32)) + vec[6]
    layer_out = layer_out.astype(BF).reshape(frames_in.shape)
    input_grad = finish(vec, x, dh, part0, near, far1).reshape(frames_in.shape)
    if ring:
        *shares, out_block = share(me, own_sum, arrived, feed_total)
        shares = [shares[0]] + [seq_swap(shares[step], step) for step in (1, 2, 3)]
        out_block = to_owners(out_block, count, 0)
        grad_qkv, grad_up, grad_down, grad_out, vectors = settle(me, shares, out_block)
        vectors = vectors.reshape(16, own)
        g_gain1, g_bias1, g_query, g_value, g_outb, g_gain2, g_bias2, g_downb = (
            vectors[i] for i in range(8)
        )
        g_upb = vectors[8:12].reshape(hid_own)
    else:
        units = fsdp_reduce(grad_heads.reshape(count, own, 3 * group)).astype(BF)
        units = units.reshape(own, 3, group)
        order = jnp.array([[0, 1, 2], [1, 0, 2], [1, 2, 0], [2, 1, 0]], jnp.int32)[s]
        got = [lax.dynamic_index_in_dim(units, order[k], 1, keepdims=False) for k in range(3)]
        got = [got[0], seq_swap(got[1], 1), seq_swap(got[2], 2)]
        odd = s % 2 == 1
        grad_qkv = jnp.concatenate(
            [jnp.where(odd, got[2], got[0]), got[1], jnp.where(odd, got[0], got[2])], 1
        ).astype(F32)
        grad_up, grad_down = feed_total[:own].astype(F32), feed_total[own:]
        out_parts = out_grads(me, [o0, o1, o2, o3], db_pieces, own)
        grad_out = to_owners(fsdp_reduce(out_parts[0]).astype(BF), count, 0).astype(F32)
        grad_down = lax.all_to_all(
            grad_down, "seq", split_axis=1, concat_axis=0, tiled=True
        ).astype(F32)
        grad_up = lax.all_to_all(
            grad_up.astype(BF).reshape(own, GROUPS, q, own), "seq", split_axis=1, concat_axis=1
        )
        grad_up = grad_up.transpose(0, 2, 1, 3).reshape(own, hidden).astype(F32)

        def placed(values, size):
            return lax.dynamic_update_slice_in_dim(
                jnp.zeros((size,), F32), values, s * values.shape[0], 0
            ).reshape(count, size // count)

        sums = [
            sums1[0].reshape(count, own),
            sums1[1].reshape(count, own),
            placed(sums1[2, :group], width),
            placed(sums1[2, 2 * group : 3 * group], width),
            sums2[0].reshape(count, own),
            sums2[1].reshape(count, own),
            sums2[2].reshape(count, own),
            sums2[3].reshape(count, own),
            lax.dynamic_update_slice_in_dim(
                jnp.zeros((count, hid_own), F32),
                (usum_a[0] + usum_b[0]).reshape(count, own),
                s * own,
                1,
            ),
        ]
        total = lax.psum(fsdp_reduce(jnp.concatenate(sums, 1)), "seq")
        g_gain1, g_bias1, g_query, g_value, g_outb, g_gain2, g_bias2, g_downb = (
            total[i * own : (i + 1) * own] for i in range(8)
        )
        g_upb = total[8 * own :]

    return (
        layer_out,
        input_grad,
        g_gain1,
        g_bias1,
        grad_qkv,
        g_query,
        g_value,
        grad_out,
        g_outb,
        g_gain2,
        g_bias2,
        grad_up,
        g_upb,
        grad_down,
        g_downb,
    )


def solution(mesh):
    tokens = P("fsdp", "seq", None)
    vector = P("fsdp")
    matrix = P("fsdp", None)
    summed = P("fsdp", "seq")
    return jax.shard_map(
        body,
        mesh=mesh,
        in_specs=(
            tokens,
            vector,
            vector,
            matrix,
            vector,
            vector,
            matrix,
            vector,
            vector,
            vector,
            matrix,
            vector,
            matrix,
            vector,
            tokens,
        ),
        out_specs=(
            tokens,
            tokens,
            vector,
            vector,
            summed,
            vector,
            vector,
            summed,
            vector,
            vector,
            vector,
            summed,
            vector,
            summed,
            vector,
        ),
        check_vma=False,
    )
```
